32 devices in a mesh: groups: 2 (over x), blk: 16 (over z, y, core).
Axes of the slice: x: 2, y: 2, z: 4, core: 2. Of those that a mesh axis runs over, the one named last changes fastest.
Arguments:
- points_in: bfloat16 [16384, 768], P(('groups', 'blk')), parts along dimension 0, may hold values from -6 to 6
- hidden_weight: bfloat16 [768, 2560], replicated, may hold values from -0.21875 to 0.21875
- output_weight: bfloat16 [2560, 768], replicated, may hold values from -0.125 to 0.125
- point_owner: int32 [16384, 1], P(('groups', 'blk')), parts along dimension 0, may hold values from 0 to 15; in each aligned block of 512 rows (0 to 511, 512 to 1023, ...) at most 64 rows name the same one
- point_node: int32 [16384], P(('groups', 'blk')), parts along dimension 0, may hold values from 0 to 31
- point_weight: int32 [16384], P(('groups', 'blk')), parts along dimension 0, may hold values from 1 to 4
- proj_weight: bfloat16 [768, 2304], replicated, may hold values from -8 to 8
- final_gain: bfloat16 [768], replicated, may hold values from 0.5 to 1.5
Outputs:
- supernodes: bfloat16 [1024, 768], P(('groups', 'blk')), parts along dimension 0
The draws below stay inside these ranges and needn't reach their ends.
There are 2 independent parts, one for each index of `groups`. The reference program is written for one: setup_inputs(seed, part) draws one part's arguments, and reference() takes and returns one part's arrays. A program takes and returns all parts, laid end to end along the dimension named above; an argument that names none is the same for every part. Nothing has to cross between parts.
Inputs may be any that keep to these rules, and one draw needn't show every extreme that they name: `point_owner`: among the 512 points of one blk index, at most 64 name the same owner, a bound that some block reaches of them.
All inputs are finite; a program needn't handle non-finite values.
Results may differ from the reference program's by a relative error of at most 0.0067.
Values may be sent and summed in bfloat16 or wider, within the bound.
No kernel may reach another device: no remote copies, remote signals or barrier semaphores. Data moves between devices by JAX's collectives and lax.ppermute only.
A program may use at most 128 MiB of HBM per device.

```python
import math
import jax
import jax.numpy as jnp
import numpy as np
from jax import lax

D = 768
HEADS = 12
FF = 2560
P_DEV = 512
S_DEV = 32
DH = 64
OWNERS = 16
CAP = 64
POINTS = 8192
NSUP = 512
N_BLK = 16


def draw_proj_weight(key, part):
    first_key = jax.random.fold_in(key, 11)
    second_key = jax.random.fold_in(key, 23)
    base = jax.random.truncated_normal(first_key, -4.0, 4.0, (D, 3 * D), jnp.float32) * D ** (-0.5)
    query_part = base[:, :D]
    factors = jax.random.permutation(second_key, jnp.arange(HEADS, dtype=jnp.int32) % 3 + 1).astype(jnp.float32)
    column_factor = jnp.repeat(factors, DH)
    query_new = column_factor[None, :] * query_part
    base = jnp.concatenate([jnp.clip(query_new, -8.0, 8.0), base[:, D:]], axis=1)
    return base.astype(jnp.bfloat16)


def touch_ends(drawn, own_key, least, largest):
    longest = drawn.shape.index(max(drawn.shape))
    spots = []
    for shift in (0, 1):
        where = [jax.random.randint(jax.random.fold_in(own_key, axis), (), 0, length) for axis, length in enumerate(drawn.shape)]
        where[longest] = (where[longest] + shift) % drawn.shape[longest]
        spots.append(tuple(where))
    return drawn.at[spots[0]].set(least).at[spots[1]].set(largest)


def steps_of(key, shape, cuts, low, high):
    level, own = 1.0, jax.random.fold_in(key, 6)
    for position, shards_of in cuts:
        draws = jnp.exp(jax.random.uniform(jax.random.fold_in(own, position), (shards_of,), jnp.float32, low / len(cuts), high / len(cuts)))
        level = level * jnp.repeat(draws, shape[position] // shards_of).reshape([-1 if axis == position else 1 for axis in range(len(shape))])
    return level


def shared_out(stream_key, own, number, rows, number_of, top, bound, lean):
    order = jax.random.permutation(stream_key, number_of)
    heavy_load, ordinary = load_shares(number_of, rows * top, bound, lean, True), load_shares(number_of, rows * top, bound, lean, False)
    places = jnp.arange(number_of)

    def named(tallies, turn):
        used = int((tallies > 0).sum())
        fixed = max(1, used // 4)
        moved = fixed + (places - fixed + turn * (used - fixed)) % max(1, number_of - fixed)
        return jnp.zeros((number_of,), jnp.int32).at[order[jnp.where(places < fixed, places, moved)]].set(jnp.asarray(tallies, jnp.int32))

    tallies = jnp.where(number % 4 == 0, named(heavy_load, number // 4), named(ordinary, number - number // 4 - 1))
    mixed = jax.random.permutation(jax.random.fold_in(own, 3), number_of)
    donor, taker = mixed[0:number_of // 2 * 2:2], mixed[1:number_of // 2 * 2:2]
    margin = jnp.minimum(tallies[donor] - 1, bound - tallies[taker]) // 2
    margin = jnp.where((donor == order[0]) | (taker == order[0]) | (tallies[taker] == 0), 0, jnp.maximum(margin, 0))
    moved = jax.random.randint(jax.random.fold_in(own, 4), (number_of // 2,), 0, 1 << 20) % (margin + 1)
    tallies = tallies.at[donor].add(-moved).at[taker].add(moved)
    members = jnp.searchsorted(jnp.cumsum(tallies), jnp.arange(rows * top), side="right").astype(jnp.int32)
    table = members.reshape(top, rows).T
    table = table[jax.random.permutation(jax.random.fold_in(own, 1), rows)]
    turn = jax.random.randint(jax.random.fold_in(own, 2), (rows, 1), 0, top)
    return jnp.take_along_axis(table, (jnp.arange(top)[None, :] + turn) % top, axis=1)


def load_shares(amount, total, reach, skew, full):
    weights = [(1 << 20) // math.isqrt(grade ** skew) + 1 for grade in range(1, amount + 1)]
    largest = reach if full else min(reach, max(-(-total // amount), total * weights[0] // sum(weights)))
    least = 1 if total - largest >= amount - 1 else 0
    holding, surplus = [largest] + [least] * (amount - 1), total - largest - least * (amount - 1)
    while surplus > 0:
        movable = [i for i in range(1, amount) if holding[i] < largest] or [i for i in range(1, amount) if holding[i] < reach]
        whole, remaining = sum([weights[i] for i in movable]), surplus
        for i in movable:
            extra = min(reach - holding[i], max(1, remaining * weights[i] // whole), surplus)
            holding[i] = holding[i] + extra
            surplus = surplus - extra
    return np.array(holding)


def normal_values(key, extent, deviation, reach, shards=(), kind=jnp.bfloat16):
    drawn = jax.random.normal(key, extent, jnp.float32) * deviation
    if len(shards) > 0:
        drawn = steps_of(key, extent, shards, -0.22, 0.18) * drawn
    return jnp.clip(drawn, min=-reach, max=reach).astype(kind)


def setup_inputs(seed: int = 0, part: int = 0) -> dict:
    seeds = jax.random.split(jax.random.key(seed), 9)
    part_keys = jax.random.split(jax.random.fold_in(seeds[8], part), 9)
    points_in = normal_values(part_keys[0], (POINTS, D), 1.0, 6.0, ((0, 16),))
    hidden_weight = normal_values(seeds[1], (D, FF), D ** -0.5, 0.21875)
    output_weight = normal_values(seeds[2], (FF, D), FF ** -0.5, 0.125)
    point_owner_keys = jax.random.split(jax.random.fold_in(part_keys[3], 1), POINTS // P_DEV)
    point_owner_turns = jax.random.permutation(jax.random.fold_in(part_keys[3], 3), POINTS // P_DEV)
    point_owner = jax.vmap(lambda own, number: shared_out(jax.random.fold_in(part_keys[3], 2), own, number, P_DEV, OWNERS, 1, CAP, 1))(point_owner_keys, point_owner_turns).reshape((POINTS, 1))
    point_node = touch_ends(jax.random.randint(part_keys[4], (POINTS,), 0, S_DEV), jax.random.fold_in(part_keys[4], 1), 0, S_DEV - 1).astype(jnp.int32)
    point_weight = touch_ends(jax.random.randint(part_keys[5], (POINTS,), 1, 5), jax.random.fold_in(part_keys[5], 1), 1, 4).astype(jnp.int32)
    proj_weight = draw_proj_weight(jax.random.fold_in(seeds[8], 71), part)
    final_gain = jnp.clip(1.0 + 0.1 * jax.random.normal(seeds[7], (D,), jnp.float32), 0.5, 1.5).astype(jnp.bfloat16)
    return dict(points_in=points_in, hidden_weight=hidden_weight, output_weight=output_weight, point_owner=point_owner, point_node=point_node, point_weight=point_weight, proj_weight=proj_weight, final_gain=final_gain)


def rms_rows(values):
    return values * lax.rsqrt(lax.optimization_barrier(jnp.mean(values * values, axis=-1, keepdims=True)) + 1e-06)

def point_block(row_block, hidden_weight, output_weight):
    normed = rms_rows(row_block.astype(jnp.float32)).astype(jnp.bfloat16)
    hidden = jax.nn.gelu(jnp.dot(normed, hidden_weight, preferred_element_type=jnp.float32), approximate=False).astype(jnp.bfloat16)
    return (row_block.astype(jnp.float32) + jnp.dot(hidden, output_weight, preferred_element_type=jnp.float32)).astype(jnp.bfloat16)

def attend_block(query_block, key_rows, value_rows):
    scores = jnp.einsum('qhd,khd->hqk', query_block.astype(jnp.float32), key_rows.astype(jnp.float32)) * DH ** (-0.5)
    highest = lax.optimization_barrier(jnp.max(scores, axis=-1, keepdims=True))
    exps = jnp.exp(scores - highest)
    weights = exps.astype(jnp.bfloat16)
    summed = jnp.einsum('hqk,khd->qhd', weights.astype(jnp.float32), value_rows.astype(jnp.float32))
    return summed / jnp.transpose(lax.optimization_barrier(jnp.sum(exps, axis=-1)))[:, :, None]

def reference(points_in, hidden_weight, output_weight, point_owner, point_node, point_weight, proj_weight, final_gain):

    def one_block(row_block):
        return point_block(row_block, hidden_weight, output_weight)
    features = lax.map(one_block, points_in.reshape(N_BLK, P_DEV, D)).reshape(POINTS, D)
    node_index = (point_owner[:, 0] * S_DEV + point_node).astype(jnp.int32)
    weight_float = point_weight.astype(jnp.float32)
    weighted = weight_float[:, None] * features.astype(jnp.float32)
    pooled_sums = jax.ops.segment_sum(weighted, node_index, num_segments=NSUP)
    totals = jax.ops.segment_sum(weight_float, node_index, num_segments=NSUP)
    pooled = pooled_sums / (1.0 + totals[:, None])
    normed_nodes = rms_rows(pooled).astype(jnp.bfloat16)
    projected = jnp.dot(normed_nodes, proj_weight, preferred_element_type=jnp.float32).astype(jnp.bfloat16)
    block_rows = math.gcd(NSUP, 512)
    queries = projected[:, :D].reshape(NSUP // block_rows, block_rows, HEADS, DH)
    key_rows = projected[:, D:2 * D].reshape(NSUP, HEADS, DH)
    value_rows = projected[:, 2 * D:].reshape(NSUP, HEADS, DH)

    def attend(query_block):
        return attend_block(query_block, key_rows, value_rows)
    attended = lax.map(attend, queries).reshape(NSUP, D)
    return (rms_rows(attended) * final_gain.astype(jnp.float32)).astype(jnp.bfloat16)
```

```python
import functools

import jax
import jax.numpy as jnp
from jax import lax
from jax.experimental import pallas as pl
from jax.experimental.pallas import tpu as pltpu
from jax.sharding import PartitionSpec as P

D = 768
HEADS = 12
S_DEV = 32
DH = 64
LANES = 128
GROUP_ROWS = 2 * S_DEV
COLS = D // LANES
TOTAL_ROWS = 16
CHUNK = COLS * GROUP_ROWS + TOTAL_ROWS
LANES_PER_GROUP = LANES // (GROUP_ROWS // TOTAL_ROWS)
MAX_TOTAL_BITS = 12
VMEM_LIMIT = 56 * 1024 * 1024


def digit_bits(devices):
    return max(1, (256 // devices).bit_length() - 1)


def gelu(values):
    return 0.5 * values * (1.0 + lax.erf(values * 0.7071067811865476))


def points_kernel(
    devices, steps, me_ref, x_ref, hidden_ref, output_ref, owner_ref, node_ref, weight_ref,
    send_ref, keep_ref, normed_ref, total_ref,
):
    step = pl.program_id(0)
    rows = x_ref.shape[0]
    part = min(rows, 256)

    @pl.when(step == 0)
    def _():
        x = x_ref[...].astype(jnp.float32)
        scale = lax.rsqrt(jnp.mean(x * x, axis=-1, keepdims=True) + 1e-06)
        normed_ref[...] = (x * scale).astype(jnp.bfloat16)
        total_ref[...] = x

    for first in range(0, rows, part):
        at = pl.ds(first, part)
        hidden = gelu(
            jnp.dot(normed_ref[at, :], hidden_ref[...], preferred_element_type=jnp.float32)
        ).astype(jnp.bfloat16)
        total_ref[at, :] += jnp.dot(hidden, output_ref[...], preferred_element_type=jnp.float32)

    @pl.when(step == steps - 1)
    def _():
        features = total_ref[...].astype(jnp.bfloat16)
        me = me_ref[0]
        owner = owner_ref[...]
        near = (owner ^ me) & (devices // 2 - 1)
        chunk_of = near // 2
        row_of = chunk_of * GROUP_ROWS + (owner // (devices // 2)) * S_DEV + node_ref[...]
        chunks = devices // 4
        half = chunks * GROUP_ROWS
        shift = digit_bits(devices)
        digits = -(-MAX_TOTAL_BITS // shift)
        lane = lax.broadcasted_iota(jnp.int32, (TOTAL_ROWS, LANES), 1)
        digit = lane % LANES_PER_GROUP
        held = jnp.where(digit < digits, digit * shift, 31)
        for core, out_ref in ((0, keep_ref), (1, send_ref)):
            place = jnp.where((near & 1) == core, row_of, -1)
            coeffs = jnp.where(
                place == lax.broadcasted_iota(jnp.int32, (half, rows), 0), weight_ref[...], 0
            ).astype(jnp.float32)
            sums = jnp.dot(
                coeffs.astype(jnp.bfloat16), features, preferred_element_type=jnp.float32
            ).astype(jnp.bfloat16)
            totals = jnp.sum(coeffs, axis=1, keepdims=True).astype(jnp.int32)
            for chunk in range(chunks):
                base = chunk * CHUNK
                first = chunk * GROUP_ROWS
                for col in range(COLS):
                    out_ref[base + col * GROUP_ROWS : base + (col + 1) * GROUP_ROWS, :] = sums[
                        first : first + GROUP_ROWS, col * LANES : (col + 1) * LANES
                    ]
                tile = jnp.zeros((TOTAL_ROWS, LANES), jnp.int32)
                for group in range(GROUP_ROWS // TOTAL_ROWS):
                    start = first + group * TOTAL_ROWS
                    value = jnp.broadcast_to(
                        totals[start : start + TOTAL_ROWS], (TOTAL_ROWS, LANES)
                    )
                    tile = jnp.where(lane // LANES_PER_GROUP == group, value, tile)
                tile = (tile >> held) & ((1 << shift) - 1)
                out_ref[base + COLS * GROUP_ROWS : base + CHUNK, :] = tile.astype(
                    jnp.float32
                ).astype(jnp.bfloat16)


def run_points(devices, me, x, hidden_weight, output_weight, owner, node, weight):
    rows, ff = x.shape[0], hidden_weight.shape[1]
    step_cols = 512
    steps = ff // step_cols
    out = jax.ShapeDtypeStruct((devices // 4 * CHUNK, LANES), jnp.bfloat16)
    whole = lambda shape: pl.BlockSpec(shape, lambda s: (0, 0))
    return pl.pallas_call(
        functools.partial(points_kernel, devices, steps),
        grid=(steps,),
        in_specs=[
            pl.BlockSpec(memory_space=pltpu.SMEM),
            whole((rows, D)),
            pl.BlockSpec((D, step_cols), lambda s: (0, s)),
            pl.BlockSpec((step_cols, D), lambda s: (s, 0)),
            whole((1, rows)),
            whole((1, rows)),
            whole((1, rows)),
        ],
        out_specs=[whole(out.shape)] * 2,
        out_shape=[out, out],
        scratch_shapes=[pltpu.VMEM((rows, D), jnp.bfloat16), pltpu.VMEM((rows, D), jnp.float32)],
        compiler_params=pltpu.CompilerParams(vmem_limit_bytes=VMEM_LIMIT),
        name="points",
    )(me, x, hidden_weight, output_weight, owner, node, weight)


def nodes_kernel(devices, mine_ref, other_ref, out_ref):
    def part(start, size):
        at = slice(start, start + size)
        return mine_ref[at, :].astype(jnp.float32) + other_ref[at, :].astype(jnp.float32)

    shift = digit_bits(devices)
    digits = -(-MAX_TOTAL_BITS // shift)
    lane = lax.broadcasted_iota(jnp.int32, (TOTAL_ROWS, LANES), 1)
    digit = lane % LANES_PER_GROUP
    worth = jnp.where(digit < digits, 1 << jnp.minimum(digit * shift, 30), 0).astype(jnp.float32)
    tile = part(COLS * GROUP_ROWS, TOTAL_ROWS) * worth
    totals = jnp.concatenate(
        [
            jnp.sum(jnp.where(lane // LANES_PER_GROUP == g, tile, 0.0), axis=1, keepdims=True)
            for g in range(GROUP_ROWS // TOTAL_ROWS)
        ],
        axis=0,
    )
    pooled = jnp.concatenate(
        [part(col * GROUP_ROWS, GROUP_ROWS) for col in range(COLS)], axis=1
    ) / (1.0 + totals)
    scale = lax.rsqrt(jnp.mean(pooled * pooled, axis=-1, keepdims=True) + 1e-06)
    out_ref[...] = (pooled * scale).astype(jnp.bfloat16)


def run_nodes(devices, mine, other):
    return pl.pallas_call(
        functools.partial(nodes_kernel, devices),
        out_shape=jax.ShapeDtypeStruct((GROUP_ROWS, D), jnp.bfloat16),
        compiler_params=pltpu.CompilerParams(vmem_limit_bytes=VMEM_LIMIT),
        name="nodes",
    )(mine, other)


def attention_kernel(first_ref, nodes_ref, proj_ref, gain_ref, out_ref):
    first = pl.multiple_of(first_ref[0], S_DEV)
    own = nodes_ref[pl.ds(first, S_DEV), :]
    queries = jnp.dot(own, proj_ref[:, :D], preferred_element_type=jnp.float32).astype(
        jnp.bfloat16
    )
    nodes = nodes_ref[...]
    keys = jnp.dot(nodes, proj_ref[:, D : 2 * D], preferred_element_type=jnp.float32).astype(
        jnp.bfloat16
    )
    values = jnp.dot(nodes, proj_ref[:, 2 * D :], preferred_element_type=jnp.float32).astype(
        jnp.bfloat16
    )
    lane = lax.broadcasted_iota(jnp.int32, (S_DEV, LANES), 1)
    low = lane < DH
    pieces = []
    for pair in range(COLS):
        at = slice(pair * LANES, (pair + 1) * LANES)
        both = queries[:, at]
        zero = jnp.zeros_like(both)
        stacked = jnp.concatenate(
            [jnp.where(low, both, zero), jnp.where(low, zero, both)], axis=0
        )
        scores = lax.dot_general(
            stacked, keys[:, at], (((1,), (1,)), ((), ())), preferred_element_type=jnp.float32
        ) * (DH**-0.5)
        exps = jnp.exp(scores - jnp.max(scores, axis=-1, keepdims=True))
        total = jnp.sum(exps, axis=-1, keepdims=True)
        summed = (
            jnp.dot(exps.astype(jnp.bfloat16), values[:, at], preferred_element_type=jnp.float32)
            / total
        )
        pieces.append(jnp.where(low, summed[:S_DEV], summed[S_DEV:]))
    attended = jnp.concatenate(pieces, axis=1)
    scale = lax.rsqrt(jnp.mean(attended * attended, axis=-1, keepdims=True) + 1e-06)
    out_ref[...] = (attended * scale * gain_ref[...].astype(jnp.float32)).astype(jnp.bfloat16)


def run_attention(first, nodes, proj_weight, gain):
    vmem = pl.BlockSpec(memory_space=pltpu.VMEM)
    return pl.pallas_call(
        attention_kernel,
        in_specs=[pl.BlockSpec(memory_space=pltpu.SMEM), vmem, vmem, vmem],
        out_specs=vmem,
        out_shape=jax.ShapeDtypeStruct((S_DEV, D), jnp.bfloat16),
        compiler_params=pltpu.CompilerParams(vmem_limit_bytes=VMEM_LIMIT),
        name="attention",
    )(first, nodes, proj_weight, gain)


def add_up(first, *rest):
    total = first.astype(jnp.float32)
    for term in rest:
        total = total + term.astype(jnp.float32)
    return total.astype(jnp.bfloat16)


def body(
    points_in,
    hidden_weight,
    output_weight,
    point_owner,
    point_node,
    point_weight,
    proj_weight,
    final_gain,
):
    rows = points_in.shape[0]
    devices = lax.axis_size("blk")
    me = lax.axis_index("blk").astype(jnp.int32)

    def swap(array, flip):
        return lax.ppermute(array, "blk", [(i, i ^ flip) for i in range(devices)])

    send, keep = run_points(
        devices,
        me.reshape(1),
        points_in,
        hidden_weight,
        output_weight,
        point_owner.reshape(1, rows),
        point_node.reshape(1, rows),
        point_weight.reshape(1, rows),
    )
    table = add_up(keep, swap(send, 1))
    groups = []
    width = (devices // 4).bit_length() - 1
    while width > 0:
        take = min(2, width)
        width -= take
        groups.append((take, width))
    for take, width in groups:
        size = (1 << width) * CHUNK
        parts = [table[j * size : (j + 1) * size] for j in range(1 << take)]
        order = list(range(1, 1 << take))[::-1]
        table = add_up(parts[0], *[swap(parts[j], j << (width + 1)) for j in order])
    nodes = run_nodes(devices, table, swap(table, devices // 2))
    for take, width in groups[::-1]:
        order = list(range(1, 1 << take))
        nodes = jnp.concatenate([nodes] + [swap(nodes, j << (width + 1)) for j in order], axis=0)
    nodes = jnp.concatenate([nodes, swap(nodes, 1)], axis=0)
    first = (me // (devices // 2) * S_DEV).reshape(1)
    return run_attention(first, nodes, proj_weight, final_gain.reshape(1, D))


def solution(mesh):
    placed = (
        P(("groups", "blk"), None),
        P(),
        P(),
        P(("groups", "blk"), None),
        P(("groups", "blk")),
        P(("groups", "blk")),
        P(),
        P(),
    )
    return jax.shard_map(
        body, mesh=mesh, in_specs=placed, out_specs=P(("groups", "blk"), None), check_vma=False
    )
```

```python
import functools

import jax
import jax.numpy as jnp
from jax import lax
from jax.experimental import pallas as pl
from jax.experimental.pallas import tpu as pltpu
from jax.sharding import PartitionSpec as P

D = 768
HEADS = 12
S_DEV = 32
DH = 64
LANES = 128
GROUP_ROWS = 2 * S_DEV
COLS = D // LANES
TOTAL_ROWS = 16
CHUNK = COLS * GROUP_ROWS + TOTAL_ROWS
LANES_PER_GROUP = LANES // (GROUP_ROWS // TOTAL_ROWS)
MIB = 1024 * 1024


def digit_bits(devices):
    return max(1, (256 // devices).bit_length() - 1)


def total_bits(rows):
    return (4 * rows).bit_length()


def gelu(values):
    return 0.5 * values * (1.0 + lax.erf(values * 0.7071067811865476))


def hidden_cols(ff):
    return 512 if ff % 512 == 0 else ff


def points_kernel(
    devices, me_ref, x_hbm, hidden_hbm, output_hbm, owner_hbm, node_hbm, weight_hbm,
    send_ref, keep_ref, owner_ref, node_ref, weight_ref, x_ref, normed_ref, hidden_ref, output_ref, coeffs_ref, middle_ref, sems,
):
    rows = x_ref.shape[0]
    ff = hidden_ref.shape[1]
    cols = hidden_cols(ff)

    def hidden_copy(part):
        at = pl.ds(pl.multiple_of(part * cols, cols), cols)
        return pltpu.make_async_copy(hidden_hbm.at[:, at], hidden_ref.at[:, at], sems.at[2 + part])

    x_copy = pltpu.make_async_copy(x_hbm, x_ref, sems.at[0])
    output_copy = pltpu.make_async_copy(output_hbm, output_ref, sems.at[1])
    index_copies = [
        pltpu.make_async_copy(source, target, sems.at[2 + ff // cols + i])
        for i, (source, target) in enumerate(
            ((owner_hbm, owner_ref), (node_hbm, node_ref), (weight_hbm, weight_ref))
        )
    ]
    for copy in index_copies:
        copy.start()
    x_copy.start()
    for part in range(ff // cols):
        hidden_copy(part).start()
    output_copy.start()

    chunks = devices // 4
    half = chunks * GROUP_ROWS
    places = [
        (out_ref, chunk * CHUNK, core * half + chunk * GROUP_ROWS)
        for core, out_ref in ((0, keep_ref), (1, send_ref))
        for chunk in range(chunks)
    ]
    me = me_ref[0]

    @pl.when(me >= 0)
    def _():
        for copy in index_copies:
            copy.wait()
        owner = owner_ref[...]
        near = (owner ^ me) & (devices // 2 - 1)
        row_of = (near // 2) * GROUP_ROWS + (owner // (devices // 2)) * S_DEV + node_ref[...]
        row_of = row_of + (near & 1) * half
        coeffs = jnp.where(
            row_of == lax.broadcasted_iota(jnp.int32, (2 * half, rows), 0), weight_ref[...], 0
        ).astype(jnp.float32)
        coeffs_ref[...] = coeffs.astype(jnp.bfloat16)
        totals = jnp.sum(coeffs, axis=1, keepdims=True).astype(jnp.int32)
        shift = digit_bits(devices)
        digits = -(-total_bits(rows) // shift)
        lane = lax.broadcasted_iota(jnp.int32, (TOTAL_ROWS, LANES), 1)
        digit = lane % LANES_PER_GROUP
        held = jnp.where(digit < digits, digit * shift, 31)
        for out_ref, base, first in places:
            tile = jnp.zeros((TOTAL_ROWS, LANES), jnp.int32)
            for group in range(GROUP_ROWS // TOTAL_ROWS):
                start = first + group * TOTAL_ROWS
                value = jnp.broadcast_to(totals[start : start + TOTAL_ROWS], (TOTAL_ROWS, LANES))
                tile = jnp.where(lane // LANES_PER_GROUP == group, value, tile)
            tile = (tile >> held) & ((1 << shift) - 1)
            out_ref[base + COLS * GROUP_ROWS : base + CHUNK, :] = tile.astype(
                jnp.float32
            ).astype(jnp.bfloat16)

    x_copy.wait()
    x = x_ref[...].astype(jnp.float32)
    scale = lax.rsqrt(jnp.mean(x * x, axis=-1, keepdims=True) + 1e-06)
    normed_ref[...] = (x * scale).astype(jnp.bfloat16)

    def one_part(part, carry):
        at = pl.ds(pl.multiple_of(part * cols, cols), cols)
        hidden_copy(part).wait()
        middle_ref[:, at] = gelu(
            jnp.dot(normed_ref[...], hidden_ref[:, at], preferred_element_type=jnp.float32)
        ).astype(jnp.bfloat16)
        return carry

    lax.fori_loop(0, ff // cols, one_part, 0)
    output_copy.wait()
    features = (
        x_ref[...].astype(jnp.float32)
        + jnp.dot(middle_ref[...], output_ref[...], preferred_element_type=jnp.float32)
    ).astype(jnp.bfloat16)
    sums = jnp.dot(coeffs_ref[...], features, preferred_element_type=jnp.float32).astype(
        jnp.bfloat16
    )
    for out_ref, base, first in places:
        for col in range(COLS):
            out_ref[base + col * GROUP_ROWS : base + (col + 1) * GROUP_ROWS, :] = sums[
                first : first + GROUP_ROWS, col * LANES : (col + 1) * LANES
            ]


def run_points(devices, me, x, hidden_weight, output_weight, owner, node, weight):
    rows, ff = x.shape[0], hidden_weight.shape[1]
    nodes = devices * S_DEV
    out = pltpu.VMEM((devices // 4 * CHUNK, LANES), jnp.bfloat16)
    hbm = pl.BlockSpec(memory_space=pl.ANY)
    vmem = pl.BlockSpec(memory_space=pltpu.VMEM)
    in_hbm = [
        pltpu.with_memory_space_constraint(array, pltpu.HBM)
        for array in (x, hidden_weight, output_weight, owner, node, weight)
    ]
    return pl.pallas_call(
        functools.partial(points_kernel, devices),
        in_specs=[pl.BlockSpec(memory_space=pltpu.SMEM)] + [hbm] * 6,
        out_specs=[vmem, vmem],
        out_shape=[out, out],
        scratch_shapes=[
            pltpu.VMEM((1, rows), jnp.int32),
            pltpu.VMEM((1, rows), jnp.int32),
            pltpu.VMEM((1, rows), jnp.int32),
            pltpu.VMEM((rows, D), jnp.bfloat16),
            pltpu.VMEM((rows, D), jnp.bfloat16),
            pltpu.VMEM((D, ff), jnp.bfloat16),
            pltpu.VMEM((ff, D), jnp.bfloat16),
            pltpu.VMEM((nodes, rows), jnp.bfloat16),
            pltpu.VMEM((rows, ff), jnp.bfloat16),
            pltpu.SemaphoreType.DMA((5 + ff // hidden_cols(ff),)),
        ],
        compiler_params=pltpu.CompilerParams(vmem_limit_bytes=28 * MIB + 8 * nodes * D),
        name="points",
    )(me, *in_hbm)


def nodes_kernel(devices, rows, mine_ref, other_ref, out_ref):
    def part(start, size):
        at = slice(start, start + size)
        return mine_ref[at, :].astype(jnp.float32) + other_ref[at, :].astype(jnp.float32)

    shift = digit_bits(devices)
    digits = -(-total_bits(rows) // shift)
    lane = lax.broadcasted_iota(jnp.int32, (TOTAL_ROWS, LANES), 1)
    digit = lane % LANES_PER_GROUP
    worth = jnp.where(digit < digits, 1 << jnp.minimum(digit * shift, 30), 0).astype(jnp.float32)
    tile = part(COLS * GROUP_ROWS, TOTAL_ROWS) * worth
    totals = jnp.concatenate(
        [
            jnp.sum(jnp.where(lane // LANES_PER_GROUP == g, tile, 0.0), axis=1, keepdims=True)
            for g in range(GROUP_ROWS // TOTAL_ROWS)
        ],
        axis=0,
    )
    pooled = jnp.concatenate(
        [part(col * GROUP_ROWS, GROUP_ROWS) for col in range(COLS)], axis=1
    ) / (1.0 + totals)
    scale = lax.rsqrt(jnp.mean(pooled * pooled, axis=-1, keepdims=True) + 1e-06)
    out_ref[...] = (pooled * scale).astype(jnp.bfloat16)


def run_nodes(devices, rows, mine, other):
    return pl.pallas_call(
        functools.partial(nodes_kernel, devices, rows),
        out_shape=pltpu.VMEM((GROUP_ROWS, D), jnp.bfloat16),
        compiler_params=pltpu.CompilerParams(vmem_limit_bytes=8 * MIB),
        name="nodes",
    )(mine, other)


def attention_kernel(first_ref, proj_ref, gain_ref, *refs):
    *pieces, out_ref, nodes_ref = refs
    first = pl.multiple_of(first_ref[0], S_DEV)
    queries = jnp.dot(
        pieces[0][pl.ds(first, S_DEV), :], proj_ref[:, :D], preferred_element_type=jnp.float32
    ).astype(jnp.bfloat16)
    start = 0
    for piece in pieces:
        nodes_ref[start : start + piece.shape[0], :] = piece[...]
        start += piece.shape[0]
    nodes = nodes_ref[...]
    keys = jnp.dot(nodes, proj_ref[:, D : 2 * D], preferred_element_type=jnp.float32).astype(
        jnp.bfloat16
    )
    values = jnp.dot(nodes, proj_ref[:, 2 * D :], preferred_element_type=jnp.float32).astype(
        jnp.bfloat16
    )
    lane = lax.broadcasted_iota(jnp.int32, (S_DEV, LANES), 1)
    low = lane < DH
    heads = []
    for pair in range(COLS):
        at = slice(pair * LANES, (pair + 1) * LANES)
        both = queries[:, at]
        zero = jnp.zeros_like(both)
        stacked = jnp.concatenate(
            [jnp.where(low, both, zero), jnp.where(low, zero, both)], axis=0
        )
        scores = lax.dot_general(
            stacked, keys[:, at], (((1,), (1,)), ((), ())), preferred_element_type=jnp.float32
        ) * (DH**-0.5)
        exps = jnp.exp(scores - jnp.max(scores, axis=-1, keepdims=True))
        total = jnp.sum(exps, axis=-1, keepdims=True)
        summed = (
            jnp.dot(exps.astype(jnp.bfloat16), values[:, at], preferred_element_type=jnp.float32)
            / total
        )
        heads.append(jnp.where(low, summed[:S_DEV], summed[S_DEV:]))
    attended = jnp.concatenate(heads, axis=1)
    scale = lax.rsqrt(jnp.mean(attended * attended, axis=-1, keepdims=True) + 1e-06)
    out_ref[...] = (attended * scale * gain_ref[...].astype(jnp.float32)).astype(jnp.bfloat16)


def run_attention(first, proj_weight, gain, pieces):
    vmem = pl.BlockSpec(memory_space=pltpu.VMEM)
    nodes = sum(piece.shape[0] for piece in pieces)
    return pl.pallas_call(
        attention_kernel,
        in_specs=[pl.BlockSpec(memory_space=pltpu.SMEM)] + [vmem] * (2 + len(pieces)),
        out_specs=vmem,
        out_shape=jax.ShapeDtypeStruct((S_DEV, D), jnp.bfloat16),
        scratch_shapes=[pltpu.VMEM((nodes, D), jnp.bfloat16)],
        compiler_params=pltpu.CompilerParams(vmem_limit_bytes=16 * MIB + 6 * nodes * D),
        name="attention",
    )(first, proj_weight, gain, *pieces)


def add_up(first, *rest):
    total = first.astype(jnp.float32)
    for term in rest:
        total = total + term.astype(jnp.float32)
    return total.astype(jnp.bfloat16)


def body(
    points_in,
    hidden_weight,
    output_weight,
    point_owner,
    point_node,
    point_weight,
    proj_weight,
    final_gain,
):
    rows = points_in.shape[0]
    devices = lax.axis_size("blk")
    me = lax.axis_index("blk").astype(jnp.int32)

    def swap(array, flip):
        return lax.ppermute(array, "blk", [(i, i ^ flip) for i in range(devices)])

    send, keep = run_points(
        devices,
        me.reshape(1),
        points_in,
        hidden_weight,
        output_weight,
        point_owner.reshape(1, rows),
        point_node.reshape(1, rows),
        point_weight.reshape(1, rows),
    )
    table = add_up(keep, swap(send, 1))
    groups = []
    width = (devices // 4).bit_length() - 1
    while width > 0:
        take = min(2, width)
        width -= take
        groups.append((take, width))
    for take, width in groups:
        size = (1 << width) * CHUNK
        parts = [table[j * size : (j + 1) * size] for j in range(1 << take)]
        order = list(range(1, 1 << take))[::-1]
        table = add_up(parts[0], *[swap(parts[j], j << (width + 1)) for j in order])
    nodes = run_nodes(devices, rows, table, swap(table, devices // 2))
    pieces = [nodes]
    for take, width in groups[::-1]:
        nodes = jnp.concatenate(pieces, axis=0)
        pieces = [nodes] + [swap(nodes, j << (width + 1)) for j in range(1, 1 << take)]
    pieces.append(swap(jnp.concatenate(pieces, axis=0), 1))
    first = (me // (devices // 2) * S_DEV).reshape(1)
    return run_attention(first, proj_weight, final_gain.reshape(1, D), pieces)


def solution(mesh):
    placed = (
        P(("groups", "blk"), None),
        P(),
        P(),
        P(("groups", "blk"), None),
        P(("groups", "blk")),
        P(("groups", "blk")),
        P(),
        P(),
    )
    return jax.shard_map(
        body, mesh=mesh, in_specs=placed, out_specs=P(("groups", "blk"), None), check_vma=False
    )
```

```python
import functools

import jax
import jax.numpy as jnp
from jax import lax
from jax.experimental import pallas as pl
from jax.experimental.pallas import tpu as pltpu
from jax.sharding import PartitionSpec as P

D = 768
HEADS = 12
S_DEV = 32
DH = 64
LANES = 128
GROUP_ROWS = 2 * S_DEV
COLS = D // LANES
TOTAL_ROWS = 16
CHUNK = COLS * GROUP_ROWS + TOTAL_ROWS
LANES_PER_GROUP = LANES // (GROUP_ROWS // TOTAL_ROWS)
MIB = 1024 * 1024


def digit_bits(devices):
    return max(1, (256 // devices).bit_length() - 1)


def total_bits(rows):
    return (4 * rows).bit_length()


def gelu(values):
    return 0.5 * values * (1.0 + lax.erf(values * 0.7071067811865476))


def hidden_cols(ff):
    return 512 if ff % 512 == 0 else ff


def points_kernel(
    devices, me_ref, x_hbm, hidden_hbm, output_hbm, owner_hbm, node_hbm, weight_hbm,
    send_ref, keep_ref, owner_ref, node_ref, weight_ref, x_ref, normed_ref, hidden_ref, output_ref, coeffs_ref, middle_ref, sems,
):
    rows = x_ref.shape[0]
    ff = hidden_ref.shape[1]
    cols = hidden_cols(ff)

    def hidden_copy(part):
        at = pl.ds(pl.multiple_of(part * cols, cols), cols)
        return pltpu.make_async_copy(hidden_hbm.at[:, at], hidden_ref.at[:, at], sems.at[2 + part])

    x_copy = pltpu.make_async_copy(x_hbm, x_ref, sems.at[0])
    output_copy = pltpu.make_async_copy(output_hbm, output_ref, sems.at[1])
    index_copies = [
        pltpu.make_async_copy(source, target, sems.at[2 + ff // cols + i])
        for i, (source, target) in enumerate(
            ((owner_hbm, owner_ref), (node_hbm, node_ref), (weight_hbm, weight_ref))
        )
    ]
    for copy in index_copies:
        copy.start()
    x_copy.start()
    for part in range(ff // cols):
        hidden_copy(part).start()
    output_copy.start()

    chunks = devices // 4
    half = chunks * GROUP_ROWS
    places = [
        (out_ref, chunk * CHUNK, core * half + chunk * GROUP_ROWS)
        for core, out_ref in ((0, keep_ref), (1, send_ref))
        for chunk in range(chunks)
    ]
    me = me_ref[0]

    @pl.when(me >= 0)
    def _():
        for copy in index_copies:
            copy.wait()
        owner = owner_ref[...]
        near = (owner ^ me) & (devices // 2 - 1)
        row_of = (near // 2) * GROUP_ROWS + (owner // (devices // 2)) * S_DEV + node_ref[...]
        row_of = row_of + (near & 1) * half
        coeffs = jnp.where(
            row_of == lax.broadcasted_iota(jnp.int32, (2 * half, rows), 0), weight_ref[...], 0
        ).astype(jnp.float32)
        coeffs_ref[...] = coeffs.astype(jnp.bfloat16)
        totals = jnp.sum(coeffs, axis=1, keepdims=True).astype(jnp.int32)
        shift = digit_bits(devices)
        digits = -(-total_bits(rows) // shift)
        lane = lax.broadcasted_iota(jnp.int32, (TOTAL_ROWS, LANES), 1)
        digit = lane % LANES_PER_GROUP
        held = jnp.where(digit < digits, digit * shift, 31)
        for out_ref, base, first in places:
            tile = jnp.zeros((TOTAL_ROWS, LANES), jnp.int32)
            for group in range(GROUP_ROWS // TOTAL_ROWS):
                start = first + group * TOTAL_ROWS
                value = jnp.broadcast_to(totals[start : start + TOTAL_ROWS], (TOTAL_ROWS, LANES))
                tile = jnp.where(lane // LANES_PER_GROUP == group, value, tile)
            tile = (tile >> held) & ((1 << shift) - 1)
            out_ref[base + COLS * GROUP_ROWS : base + CHUNK, :] = tile.astype(
                jnp.float32
            ).astype(jnp.bfloat16)

    x_copy.wait()
    x = x_ref[...].astype(jnp.float32)
    scale = lax.rsqrt(jnp.mean(x * x, axis=-1, keepdims=True) + 1e-06)
    normed_ref[...] = (x * scale).astype(jnp.bfloat16)

    def one_part(part, carry):
        at = pl.ds(pl.multiple_of(part * cols, cols), cols)
        hidden_copy(part).wait()
        middle_ref[:, at] = gelu(
            jnp.dot(normed_ref[...], hidden_ref[:, at], preferred_element_type=jnp.float32)
        ).astype(jnp.bfloat16)
        return carry

    lax.fori_loop(0, ff // cols, one_part, 0)
    output_copy.wait()
    features = (
        x_ref[...].astype(jnp.float32)
        + jnp.dot(middle_ref[...], output_ref[...], preferred_element_type=jnp.float32)
    ).astype(jnp.bfloat16)
    sums = jnp.dot(coeffs_ref[...], features, preferred_element_type=jnp.float32).astype(
        jnp.bfloat16
    )
    for out_ref, base, first in places:
        for col in range(COLS):
            out_ref[base + col * GROUP_ROWS : base + (col + 1) * GROUP_ROWS, :] = sums[
                first : first + GROUP_ROWS, col * LANES : (col + 1) * LANES
            ]


def run_points(devices, me, x, hidden_weight, output_weight, owner, node, weight):
    rows, ff = x.shape[0], hidden_weight.shape[1]
    nodes = devices * S_DEV
    out = pltpu.VMEM((devices // 4 * CHUNK, LANES), jnp.bfloat16)
    hbm = pl.BlockSpec(memory_space=pl.ANY)
    vmem = pl.BlockSpec(memory_space=pltpu.VMEM)
    in_hbm = [
        pltpu.with_memory_space_constraint(array, pltpu.HBM)
        for array in (x, hidden_weight, output_weight, owner, node, weight)
    ]
    return pl.pallas_call(
        functools.partial(points_kernel, devices),
        in_specs=[pl.BlockSpec(memory_space=pltpu.SMEM)] + [hbm] * 6,
        out_specs=[vmem, vmem],
        out_shape=[out, out],
        scratch_shapes=[
            pltpu.VMEM((1, rows), jnp.int32),
            pltpu.VMEM((1, rows), jnp.int32),
            pltpu.VMEM((1, rows), jnp.int32),
            pltpu.VMEM((rows, D), jnp.bfloat16),
            pltpu.VMEM((rows, D), jnp.bfloat16),
            pltpu.VMEM((D, ff), jnp.bfloat16),
            pltpu.VMEM((ff, D), jnp.bfloat16),
            pltpu.VMEM((nodes, rows), jnp.bfloat16),
            pltpu.VMEM((rows, ff), jnp.bfloat16),
            pltpu.SemaphoreType.DMA((5 + ff // hidden_cols(ff),)),
        ],
        compiler_params=pltpu.CompilerParams(vmem_limit_bytes=28 * MIB + 8 * nodes * D),
        name="points",
    )(me, *in_hbm)


def nodes_kernel(devices, rows, mine_ref, other_ref, out_ref):
    def part(start, size):
        at = slice(start, start + size)
        return mine_ref[at, :].astype(jnp.float32) + other_ref[at, :].astype(jnp.float32)

    shift = digit_bits(devices)
    digits = -(-total_bits(rows) // shift)
    lane = lax.broadcasted_iota(jnp.int32, (TOTAL_ROWS, LANES), 1)
    digit = lane % LANES_PER_GROUP
    worth = jnp.where(digit < digits, 1 << jnp.minimum(digit * shift, 30), 0).astype(jnp.float32)
    tile = part(COLS * GROUP_ROWS, TOTAL_ROWS) * worth
    totals = jnp.concatenate(
        [
            jnp.sum(jnp.where(lane // LANES_PER_GROUP == g, tile, 0.0), axis=1, keepdims=True)
            for g in range(GROUP_ROWS // TOTAL_ROWS)
        ],
        axis=0,
    )
    pooled = jnp.concatenate(
        [part(col * GROUP_ROWS, GROUP_ROWS) for col in range(COLS)], axis=1
    ) / (1.0 + totals)
    scale = lax.rsqrt(jnp.mean(pooled * pooled, axis=-1, keepdims=True) + 1e-06)
    out_ref[...] = (pooled * scale).astype(jnp.bfloat16)


def run_nodes(devices, rows, mine, other):
    return pl.pallas_call(
        functools.partial(nodes_kernel, devices, rows),
        out_shape=pltpu.VMEM((GROUP_ROWS, D), jnp.bfloat16),
        compiler_params=pltpu.CompilerParams(vmem_limit_bytes=8 * MIB),
        name="nodes",
    )(*in_vmem(mine, other))


def in_vmem(*arrays):
    return [pltpu.with_memory_space_constraint(array, pltpu.VMEM) for array in arrays]


def join_kernel(*refs):
    *pieces, out_ref = refs
    start = 0
    for piece in pieces:
        out_ref[start : start + piece.shape[0], :] = piece[...]
        start += piece.shape[0]


def run_join(pieces):
    rows = sum(piece.shape[0] for piece in pieces)
    return pl.pallas_call(
        join_kernel,
        out_shape=pltpu.VMEM((rows, D), jnp.bfloat16),
        compiler_params=pltpu.CompilerParams(vmem_limit_bytes=8 * MIB),
        name="join",
    )(*in_vmem(*pieces))


def project(rows, proj_ref, start, size):
    return jnp.dot(
        rows, proj_ref[:, start : start + size], preferred_element_type=jnp.float32
    ).astype(jnp.bfloat16)


def project_kernel(first_ref, nodes_ref, proj_ref, query_ref, key_value_ref):
    first = pl.multiple_of(first_ref[0], S_DEV)
    query_ref[...] = project(nodes_ref[pl.ds(first, S_DEV), :], proj_ref, 0, D)
    key_value_ref[...] = project(nodes_ref[...], proj_ref, D, 2 * D)


def run_project(first, nodes, proj_weight):
    rows = nodes.shape[0]
    return pl.pallas_call(
        project_kernel,
        in_specs=[pl.BlockSpec(memory_space=pltpu.SMEM)]
        + [pl.BlockSpec(memory_space=pltpu.VMEM)] * 2,
        out_shape=[
            pltpu.VMEM((S_DEV, D), jnp.bfloat16),
            pltpu.VMEM((rows, 2 * D), jnp.bfloat16),
        ],
        compiler_params=pltpu.CompilerParams(vmem_limit_bytes=8 * MIB + 16 * rows * D),
        cost_estimate=pl.CostEstimate(
            flops=4 * rows * D * D, bytes_accessed=6 * D * D + 6 * rows * D, transcendentals=0
        ),
        name="project",
    )(first, *in_vmem(nodes, proj_weight))


def attention_kernel(query_ref, near_ref, nodes_ref, proj_ref, gain_ref, out_ref):
    far = project(nodes_ref[...], proj_ref, D, 2 * D)
    keys = jnp.concatenate([near_ref[:, :D], far[:, :D]], axis=0)
    values = jnp.concatenate([near_ref[:, D:], far[:, D:]], axis=0)
    queries = query_ref[...]
    lane = lax.broadcasted_iota(jnp.int32, (S_DEV, LANES), 1)
    low = lane < DH
    heads = []
    for pair in range(COLS):
        at = slice(pair * LANES, (pair + 1) * LANES)
        both = queries[:, at]
        zero = jnp.zeros_like(both)
        stacked = jnp.concatenate(
            [jnp.where(low, both, zero), jnp.where(low, zero, both)], axis=0
        )
        scores = lax.dot_general(
            stacked, keys[:, at], (((1,), (1,)), ((), ())), preferred_element_type=jnp.float32
        ) * (DH**-0.5)
        exps = jnp.exp(scores - jnp.max(scores, axis=-1, keepdims=True))
        total = jnp.sum(exps, axis=-1, keepdims=True)
        summed = (
            jnp.dot(exps.astype(jnp.bfloat16), values[:, at], preferred_element_type=jnp.float32)
            / total
        )
        heads.append(jnp.where(low, summed[:S_DEV], summed[S_DEV:]))
    attended = jnp.concatenate(heads, axis=1)
    scale = lax.rsqrt(jnp.mean(attended * attended, axis=-1, keepdims=True) + 1e-06)
    out_ref[...] = (attended * scale * gain_ref[...].astype(jnp.float32)).astype(jnp.bfloat16)


def run_attention(query, near, nodes, proj_weight, gain):
    rows = nodes.shape[0]
    return pl.pallas_call(
        attention_kernel,
        out_shape=jax.ShapeDtypeStruct((S_DEV, D), jnp.bfloat16),
        compiler_params=pltpu.CompilerParams(vmem_limit_bytes=16 * MIB + 16 * rows * D),
        name="attention",
    )(*in_vmem(query, near, nodes, proj_weight), gain)


def add_up(first, *rest):
    total = first.astype(jnp.float32)
    for term in rest:
        total = total + term.astype(jnp.float32)
    return total.astype(jnp.bfloat16)


def body(
    points_in,
    hidden_weight,
    output_weight,
    point_owner,
    point_node,
    point_weight,
    proj_weight,
    final_gain,
):
    rows = points_in.shape[0]
    devices = lax.axis_size("blk")
    me = lax.axis_index("blk").astype(jnp.int32)

    def swap(array, flip):
        return lax.ppermute(array, "blk", [(i, i ^ flip) for i in range(devices)])

    send, keep = run_points(
        devices,
        me.reshape(1),
        points_in,
        hidden_weight,
        output_weight,
        point_owner.reshape(1, rows),
        point_node.reshape(1, rows),
        point_weight.reshape(1, rows),
    )
    table = add_up(keep, swap(send, 1))
    groups = []
    width = (devices // 4).bit_length() - 1
    while width > 0:
        take = min(2, width)
        width -= take
        groups.append((take, width))
    for take, width in groups:
        size = (1 << width) * CHUNK
        parts = [table[j * size : (j + 1) * size] for j in range(1 << take)]
        order = list(range(1, 1 << take))[::-1]
        table = add_up(parts[0], *[swap(parts[j], j << (width + 1)) for j in order])
    nodes = run_nodes(devices, rows, table, swap(table, devices // 2))
    for take, width in groups[::-1]:
        nodes = run_join([nodes] + [swap(nodes, j << (width + 1)) for j in range(1, 1 << take)])
    other = swap(nodes, 1)
    first = (me // (devices // 2) * S_DEV).reshape(1)
    query, near = run_project(first, nodes, proj_weight)
    return run_attention(query, near, other, proj_weight, final_gain.reshape(1, D))


def solution(mesh):
    placed = (
        P(("groups", "blk"), None),
        P(),
        P(),
        P(("groups", "blk"), None),
        P(("groups", "blk")),
        P(("groups", "blk")),
        P(),
        P(),
    )
    return jax.shard_map(
        body, mesh=mesh, in_specs=placed, out_specs=P(("groups", "blk"), None), check_vma=False
    )
```

```python
import functools

import jax
import jax.numpy as jnp
from jax import lax
from jax.experimental import pallas as pl
from jax.experimental.pallas import tpu as pltpu
from jax.sharding import PartitionSpec as P

D = 768
HEADS = 12
S_DEV = 32
DH = 64
LANES = 128
GROUP_ROWS = 2 * S_DEV
COLS = D // LANES
TOTAL_ROWS = 16
CHUNK = COLS * GROUP_ROWS + TOTAL_ROWS
LANES_PER_GROUP = LANES // (GROUP_ROWS // TOTAL_ROWS)
MIB = 1024 * 1024


def digit_bits(devices):
    return max(1, (256 // devices).bit_length() - 1)


def total_bits(rows):
    return (4 * rows).bit_length()


def gelu(values):
    return 0.5 * values * (1.0 + lax.erf(values * 0.7071067811865476))


def hidden_parts(ff):
    stops = [stop for stop in (256, 1024) if stop < ff] + [ff]
    return [slice(start, stop) for start, stop in zip([0] + stops[:-1], stops)]


def points_kernel(
    devices, me_ref, x_hbm, hidden_hbm, output_hbm, owner_hbm, node_hbm, weight_hbm,
    send_ref, keep_ref, owner_ref, node_ref, weight_ref, x_ref, normed_ref, hidden_ref, output_ref, coeffs_ref, middle_ref, sems,
):
    rows = x_ref.shape[0]
    ff = hidden_ref.shape[1]
    parts = hidden_parts(ff)

    def hidden_copy(part):
        at = parts[part]
        return pltpu.make_async_copy(hidden_hbm.at[:, at], hidden_ref.at[:, at], sems.at[2 + part])

    x_copy = pltpu.make_async_copy(x_hbm, x_ref, sems.at[0])
    output_copy = pltpu.make_async_copy(output_hbm, output_ref, sems.at[1])
    index_copies = [
        pltpu.make_async_copy(source, target, sems.at[2 + len(parts) + i])
        for i, (source, target) in enumerate(
            ((owner_hbm, owner_ref), (node_hbm, node_ref), (weight_hbm, weight_ref))
        )
    ]
    for copy in index_copies:
        copy.start()
    x_copy.start()
    for part in range(len(parts)):
        hidden_copy(part).start()
    output_copy.start()

    chunks = devices // 4
    half = chunks * GROUP_ROWS
    places = [
        (out_ref, chunk * CHUNK, core * half + chunk * GROUP_ROWS)
        for core, out_ref in ((0, keep_ref), (1, send_ref))
        for chunk in range(chunks)
    ]
    me = me_ref[0]

    @pl.when(me >= 0)
    def _():
        for copy in index_copies:
            copy.wait()
        owner = owner_ref[...]
        near = (owner ^ me) & (devices // 2 - 1)
        row_of = (near // 2) * GROUP_ROWS + (owner // (devices // 2)) * S_DEV + node_ref[...]
        row_of = row_of + (near & 1) * half
        coeffs = jnp.where(
            row_of == lax.broadcasted_iota(jnp.int32, (2 * half, rows), 0), weight_ref[...], 0
        ).astype(jnp.float32)
        coeffs_ref[...] = coeffs.astype(jnp.bfloat16)
        totals = jnp.sum(coeffs, axis=1, keepdims=True).astype(jnp.int32)
        shift = digit_bits(devices)
        digits = -(-total_bits(rows) // shift)
        lane = lax.broadcasted_iota(jnp.int32, (TOTAL_ROWS, LANES), 1)
        digit = lane % LANES_PER_GROUP
        held = jnp.where(digit < digits, digit * shift, 31)
        for out_ref, base, first in places:
            tile = jnp.zeros((TOTAL_ROWS, LANES), jnp.int32)
            for group in range(GROUP_ROWS // TOTAL_ROWS):
                start = first + group * TOTAL_ROWS
                value = jnp.broadcast_to(totals[start : start + TOTAL_ROWS], (TOTAL_ROWS, LANES))
                tile = jnp.where(lane // LANES_PER_GROUP == group, value, tile)
            tile = (tile >> held) & ((1 << shift) - 1)
            out_ref[base + COLS * GROUP_ROWS : base + CHUNK, :] = tile.astype(
                jnp.float32
            ).astype(jnp.bfloat16)

    x_copy.wait()
    x = x_ref[...].astype(jnp.float32)
    scale = lax.rsqrt(jnp.mean(x * x, axis=-1, keepdims=True) + 1e-06)
    normed_ref[...] = (x * scale).astype(jnp.bfloat16)

    def one_part(part):
        at = parts[part]

        @pl.when(me >= 0)
        def _():
            hidden_copy(part).wait()
            middle_ref[:, at] = gelu(
                jnp.dot(normed_ref[...], hidden_ref[:, at], preferred_element_type=jnp.float32)
            ).astype(jnp.bfloat16)

    for part in range(len(parts)):
        one_part(part)
    output_copy.wait()
    features = (
        x_ref[...].astype(jnp.float32)
        + jnp.dot(middle_ref[...], output_ref[...], preferred_element_type=jnp.float32)
    ).astype(jnp.bfloat16)
    sums = jnp.dot(coeffs_ref[...], features, preferred_element_type=jnp.float32).astype(
        jnp.bfloat16
    )
    for out_ref, base, first in places:
        for col in range(COLS):
            out_ref[base + col * GROUP_ROWS : base + (col + 1) * GROUP_ROWS, :] = sums[
                first : first + GROUP_ROWS, col * LANES : (col + 1) * LANES
            ]


def run_points(devices, me, x, hidden_weight, output_weight, owner, node, weight):
    rows, ff = x.shape[0], hidden_weight.shape[1]
    nodes = devices * S_DEV
    out = pltpu.VMEM((devices // 4 * CHUNK, LANES), jnp.bfloat16)
    hbm = pl.BlockSpec(memory_space=pl.ANY)
    vmem = pl.BlockSpec(memory_space=pltpu.VMEM)
    in_hbm = [
        pltpu.with_memory_space_constraint(array, pltpu.HBM)
        for array in (x, hidden_weight, output_weight, owner, node, weight)
    ]
    return pl.pallas_call(
        functools.partial(points_kernel, devices),
        in_specs=[pl.BlockSpec(memory_space=pltpu.SMEM)] + [hbm] * 6,
        out_specs=[vmem, vmem],
        out_shape=[out, out],
        scratch_shapes=[
            pltpu.VMEM((1, rows), jnp.int32),
            pltpu.VMEM((1, rows), jnp.int32),
            pltpu.VMEM((1, rows), jnp.int32),
            pltpu.VMEM((rows, D), jnp.bfloat16),
            pltpu.VMEM((rows, D), jnp.bfloat16),
            pltpu.VMEM((D, ff), jnp.bfloat16),
            pltpu.VMEM((ff, D), jnp.bfloat16),
            pltpu.VMEM((nodes, rows), jnp.bfloat16),
            pltpu.VMEM((rows, ff), jnp.bfloat16),
            pltpu.SemaphoreType.DMA((5 + len(hidden_parts(ff)),)),
        ],
        compiler_params=pltpu.CompilerParams(vmem_limit_bytes=28 * MIB + 8 * nodes * D),
        name="points",
    )(me, *in_hbm)


def nodes_kernel(devices, rows, me_ref, mine_ref, other_ref, out_ref, own_ref):
    def part(start, size):
        at = slice(start, start + size)
        return mine_ref[at, :].astype(jnp.float32) + other_ref[at, :].astype(jnp.float32)

    shift = digit_bits(devices)
    digits = -(-total_bits(rows) // shift)
    lane = lax.broadcasted_iota(jnp.int32, (TOTAL_ROWS, LANES), 1)
    digit = lane % LANES_PER_GROUP
    worth = jnp.where(digit < digits, 1 << jnp.minimum(digit * shift, 30), 0).astype(jnp.float32)
    tile = part(COLS * GROUP_ROWS, TOTAL_ROWS) * worth
    totals = jnp.concatenate(
        [
            jnp.sum(jnp.where(lane // LANES_PER_GROUP == g, tile, 0.0), axis=1, keepdims=True)
            for g in range(GROUP_ROWS // TOTAL_ROWS)
        ],
        axis=0,
    )
    pooled = jnp.concatenate(
        [part(col * GROUP_ROWS, GROUP_ROWS) for col in range(COLS)], axis=1
    ) / (1.0 + totals)
    scale = lax.rsqrt(jnp.mean(pooled * pooled, axis=-1, keepdims=True) + 1e-06)
    out_ref[...] = (pooled * scale).astype(jnp.bfloat16)
    first = me_ref[0] // (devices // 2) * S_DEV
    own_ref[...] = out_ref[pl.ds(pl.multiple_of(first, S_DEV), S_DEV), :]


def run_nodes(devices, rows, me, mine, other):
    return pl.pallas_call(
        functools.partial(nodes_kernel, devices, rows),
        in_specs=[pl.BlockSpec(memory_space=pltpu.SMEM)]
        + [pl.BlockSpec(memory_space=pltpu.VMEM)] * 2,
        out_shape=[
            pltpu.VMEM((GROUP_ROWS, D), jnp.bfloat16),
            pltpu.VMEM((S_DEV, D), jnp.bfloat16),
        ],
        compiler_params=pltpu.CompilerParams(vmem_limit_bytes=8 * MIB),
        name="nodes",
    )(me, *in_vmem(mine, other))


def in_vmem(*arrays):
    return [pltpu.with_memory_space_constraint(array, pltpu.VMEM) for array in arrays]


def project(rows, proj_ref, start, size):
    return jnp.dot(
        rows, proj_ref[:, start : start + size], preferred_element_type=jnp.float32
    ).astype(jnp.bfloat16)


def partial_kernel(own_ref, other_ref, proj_ref, *refs):
    *pieces, mine_ref, theirs_ref, nodes_ref = refs
    start = 0
    for piece in pieces:
        nodes_ref[start : start + piece.shape[0], :] = piece[...]
        start += piece.shape[0]
    queries = project(
        jnp.concatenate([own_ref[...], other_ref[...]], axis=0), proj_ref, 0, D
    )
    keys = project(nodes_ref[...], proj_ref, D, D)
    values = project(nodes_ref[...], proj_ref, 2 * D, D)
    rows = 2 * S_DEV
    lane = lax.broadcasted_iota(jnp.int32, (rows, LANES), 1)
    low = lane < DH
    stats = jnp.zeros((rows, LANES), jnp.float32)
    for pair in range(COLS):
        at = slice(pair * LANES, (pair + 1) * LANES)
        both = queries[:, at]
        zero = jnp.zeros_like(both)
        stacked = jnp.concatenate(
            [jnp.where(low, both, zero), jnp.where(low, zero, both)], axis=0
        )
        scores = lax.dot_general(
            stacked, keys[:, at], (((1,), (1,)), ((), ())), preferred_element_type=jnp.float32
        ) * (DH**-0.5)
        highest = jnp.max(scores, axis=-1, keepdims=True)
        exps = jnp.exp(scores - highest)
        total = jnp.sum(exps, axis=-1, keepdims=True)
        summed = jnp.dot(
            exps.astype(jnp.bfloat16), values[:, at], preferred_element_type=jnp.float32
        )
        for half in (0, 1):
            these = slice(half * rows, (half + 1) * rows)
            stats = jnp.where(lane == 2 * pair + half, highest[these], stats)
            stats = jnp.where(lane == DH + 2 * pair + half, total[these], stats)
        piece = jnp.where(low, summed[:rows], summed[rows:])
        mine_ref[:, at] = piece[:S_DEV]
        theirs_ref[:, at] = piece[S_DEV:]
    mine_ref[:, D:] = stats[:S_DEV]
    theirs_ref[:, D:] = stats[S_DEV:]


def run_partial(own, other, proj_weight, pieces):
    rows = sum(piece.shape[0] for piece in pieces)
    out = pltpu.VMEM((S_DEV, D + LANES), jnp.float32)
    return pl.pallas_call(
        partial_kernel,
        out_shape=[out, out],
        scratch_shapes=[pltpu.VMEM((rows, D), jnp.bfloat16)],
        compiler_params=pltpu.CompilerParams(vmem_limit_bytes=12 * MIB + 24 * rows * D),
        name="partial",
    )(*in_vmem(own, other, proj_weight, *pieces))


def merge_kernel(mine_ref, theirs_ref, gain_ref, out_ref):
    mine, theirs = mine_ref[:, D:], theirs_ref[:, D:]
    highest = jnp.maximum(mine, theirs)
    mine_scale, theirs_scale = jnp.exp(mine - highest), jnp.exp(theirs - highest)
    mine_total = pltpu.roll(mine, DH, 1)
    theirs_total = pltpu.roll(theirs, DH, 1)
    total = mine_total * mine_scale + theirs_total * theirs_scale
    mine_scale, theirs_scale = mine_scale / total, theirs_scale / total
    low = lax.broadcasted_iota(jnp.int32, (S_DEV, LANES), 1) < DH
    heads = []
    for pair in range(COLS):
        at = slice(pair * LANES, (pair + 1) * LANES)
        first, second = slice(2 * pair, 2 * pair + 1), slice(2 * pair + 1, 2 * pair + 2)
        heads.append(
            mine_ref[:, at] * jnp.where(low, mine_scale[:, first], mine_scale[:, second])
            + theirs_ref[:, at] * jnp.where(low, theirs_scale[:, first], theirs_scale[:, second])
        )
    attended = jnp.concatenate(heads, axis=1)
    scale = lax.rsqrt(jnp.mean(attended * attended, axis=-1, keepdims=True) + 1e-06)
    out_ref[...] = (attended * scale * gain_ref[...].astype(jnp.float32)).astype(jnp.bfloat16)


def run_merge(mine, theirs, gain):
    return pl.pallas_call(
        merge_kernel,
        out_shape=jax.ShapeDtypeStruct((S_DEV, D), jnp.bfloat16),
        compiler_params=pltpu.CompilerParams(vmem_limit_bytes=8 * MIB),
        name="merge",
    )(*in_vmem(mine, theirs), gain)


def add_up(first, *rest):
    total = first.astype(jnp.float32)
    for term in rest:
        total = total + term.astype(jnp.float32)
    return total.astype(jnp.bfloat16)


def body(
    points_in,
    hidden_weight,
    output_weight,
    point_owner,
    point_node,
    point_weight,
    proj_weight,
    final_gain,
):
    rows = points_in.shape[0]
    devices = lax.axis_size("blk")
    me = lax.axis_index("blk").astype(jnp.int32).reshape(1)

    def swap(array, flip):
        return lax.ppermute(array, "blk", [(i, i ^ flip) for i in range(devices)])

    send, keep = run_points(
        devices,
        me,
        points_in,
        hidden_weight,
        output_weight,
        point_owner.reshape(1, rows),
        point_node.reshape(1, rows),
        point_weight.reshape(1, rows),
    )
    table = add_up(keep, swap(send, 1))
    groups = []
    width = (devices // 4).bit_length() - 1
    while width > 0:
        take = min(2, width)
        width -= take
        groups.append((take, width))
    for take, width in groups:
        size = (1 << width) * CHUNK
        parts = [table[j * size : (j + 1) * size] for j in range(1 << take)]
        order = list(range(1, 1 << take))[::-1]
        table = add_up(parts[0], *[swap(parts[j], j << (width + 1)) for j in order])
    nodes, own = run_nodes(devices, rows, me, table, swap(table, devices // 2))
    pieces = [nodes]
    for take, width in groups[::-1]:
        pieces += [
            swap(piece, j << (width + 1))
            for j in range((1 << take) - 1, 0, -1)
            for piece in pieces
        ]
    pieces[1], held = lax.optimization_barrier((pieces[1], own))
    other = swap(held, 1)
    mine, theirs = run_partial(own, other, proj_weight, pieces)
    return run_merge(mine, swap(theirs, 1), final_gain.reshape(1, D))


def solution(mesh):
    placed = (
        P(("groups", "blk"), None),
        P(),
        P(),
        P(("groups", "blk"), None),
        P(("groups", "blk")),
        P(("groups", "blk")),
        P(),
        P(),
    )
    return jax.shard_map(
        body, mesh=mesh, in_specs=placed, out_specs=P(("groups", "blk"), None), check_vma=False
    )
```

```python
import functools

import jax
import jax.numpy as jnp
from jax import lax
from jax.experimental import pallas as pl
from jax.experimental.pallas import tpu as pltpu
from jax.sharding import PartitionSpec as P

D = 768
HEADS = 12
S_DEV = 32
DH = 64
LANES = 128
GROUP_ROWS = 2 * S_DEV
COLS = D // LANES
TOTAL_ROWS = 16
CHUNK = COLS * GROUP_ROWS + TOTAL_ROWS
LANES_PER_GROUP = LANES // (GROUP_ROWS // TOTAL_ROWS)
MIB = 1024 * 1024


def digit_bits(devices):
    return max(1, (256 // devices).bit_length() - 1)


def total_bits(rows):
    return (4 * rows).bit_length()


def gelu(values):
    return 0.5 * values * (1.0 + lax.erf(values * 0.7071067811865476))


def hidden_parts(ff):
    stops = [stop for stop in (768,) if stop < ff] + [ff]
    return [slice(start, stop) for start, stop in zip([0] + stops[:-1], stops)]


def points_kernel(
    devices, me_ref, x_hbm, hidden_hbm, output_hbm, owner_hbm, node_hbm, weight_hbm,
    send_ref, keep_ref, owner_ref, node_ref, weight_ref, x_ref, normed_ref, hidden_ref, output_ref, coeffs_ref, middle_ref, sems,
):
    rows = x_ref.shape[0]
    ff = hidden_ref.shape[1]
    parts = hidden_parts(ff)

    def hidden_copy(part):
        at = parts[part]
        return pltpu.make_async_copy(hidden_hbm.at[:, at], hidden_ref.at[:, at], sems.at[2 + part])

    x_copy = pltpu.make_async_copy(x_hbm, x_ref, sems.at[0])
    output_copy = pltpu.make_async_copy(output_hbm, output_ref, sems.at[1])
    index_copies = [
        pltpu.make_async_copy(source, target, sems.at[2 + len(parts) + i])
        for i, (source, target) in enumerate(
            ((owner_hbm, owner_ref), (node_hbm, node_ref), (weight_hbm, weight_ref))
        )
    ]
    for copy in index_copies:
        copy.start()
    x_copy.start()
    for part in range(len(parts)):
        hidden_copy(part).start()
    output_copy.start()

    chunks = devices // 4
    half = chunks * GROUP_ROWS
    places = [
        (out_ref, chunk * CHUNK, core * half + chunk * GROUP_ROWS)
        for core, out_ref in ((0, keep_ref), (1, send_ref))
        for chunk in range(chunks)
    ]
    me = me_ref[0]

    @pl.when(me >= 0)
    def _():
        for copy in index_copies:
            copy.wait()
        owner = owner_ref[...]
        near = (owner ^ me) & (devices // 2 - 1)
        row_of = (near // 2) * GROUP_ROWS + (owner // (devices // 2)) * S_DEV + node_ref[...]
        row_of = row_of + (near & 1) * half
        coeffs = jnp.where(
            row_of == lax.broadcasted_iota(jnp.int32, (2 * half, rows), 0), weight_ref[...], 0
        ).astype(jnp.float32)
        coeffs_ref[...] = coeffs.astype(jnp.bfloat16)
        totals = jnp.sum(coeffs, axis=1, keepdims=True).astype(jnp.int32)
        shift = digit_bits(devices)
        digits = -(-total_bits(rows) // shift)
        lane = lax.broadcasted_iota(jnp.int32, (TOTAL_ROWS, LANES), 1)
        digit = lane % LANES_PER_GROUP
        held = jnp.where(digit < digits, digit * shift, 31)
        for out_ref, base, first in places:
            tile = jnp.zeros((TOTAL_ROWS, LANES), jnp.int32)
            for group in range(GROUP_ROWS // TOTAL_ROWS):
                start = first + group * TOTAL_ROWS
                value = jnp.broadcast_to(totals[start : start + TOTAL_ROWS], (TOTAL_ROWS, LANES))
                tile = jnp.where(lane // LANES_PER_GROUP == group, value, tile)
            tile = (tile >> held) & ((1 << shift) - 1)
            out_ref[base + COLS * GROUP_ROWS : base + CHUNK, :] = tile.astype(
                jnp.float32
            ).astype(jnp.bfloat16)

    x_copy.wait()
    x = x_ref[...].astype(jnp.float32)
    scale = lax.rsqrt(jnp.mean(x * x, axis=-1, keepdims=True) + 1e-06)
    normed_ref[...] = (x * scale).astype(jnp.bfloat16)

    def one_part(part):
        at = parts[part]

        @pl.when(me > -2 - part)
        def _():
            hidden_copy(part).wait()
            middle_ref[:, at] = gelu(
                jnp.dot(normed_ref[...], hidden_ref[:, at], preferred_element_type=jnp.float32)
            ).astype(jnp.bfloat16)

    for part in range(len(parts)):
        one_part(part)
    output_copy.wait()
    sums = None
    half_rows = rows // 2
    for at in (slice(0, half_rows), slice(half_rows, rows)):
        features = (
            x_ref[at, :].astype(jnp.float32)
            + jnp.dot(middle_ref[at, :], output_ref[...], preferred_element_type=jnp.float32)
        ).astype(jnp.bfloat16)
        term = jnp.dot(coeffs_ref[:, at], features, preferred_element_type=jnp.float32)
        sums = term if sums is None else sums + term
    sums = sums.astype(jnp.bfloat16)
    for out_ref, base, first in places:
        for col in range(COLS):
            out_ref[base + col * GROUP_ROWS : base + (col + 1) * GROUP_ROWS, :] = sums[
                first : first + GROUP_ROWS, col * LANES : (col + 1) * LANES
            ]


def run_points(devices, me, x, hidden_weight, output_weight, owner, node, weight):
    rows, ff = x.shape[0], hidden_weight.shape[1]
    nodes = devices * S_DEV
    out = pltpu.VMEM((devices // 4 * CHUNK, LANES), jnp.bfloat16)
    hbm = pl.BlockSpec(memory_space=pl.ANY)
    vmem = pl.BlockSpec(memory_space=pltpu.VMEM)
    in_hbm = [
        pltpu.with_memory_space_constraint(array, pltpu.HBM)
        for array in (x, hidden_weight, output_weight, owner, node, weight)
    ]
    return pl.pallas_call(
        functools.partial(points_kernel, devices),
        in_specs=[pl.BlockSpec(memory_space=pltpu.SMEM)] + [hbm] * 6,
        out_specs=[vmem, vmem],
        out_shape=[out, out],
        scratch_shapes=[
            pltpu.VMEM((1, rows), jnp.int32),
            pltpu.VMEM((1, rows), jnp.int32),
            pltpu.VMEM((1, rows), jnp.int32),
            pltpu.VMEM((rows, D), jnp.bfloat16),
            pltpu.VMEM((rows, D), jnp.bfloat16),
            pltpu.VMEM((D, ff), jnp.bfloat16),
            pltpu.VMEM((ff, D), jnp.bfloat16),
            pltpu.VMEM((nodes, rows), jnp.bfloat16),
            pltpu.VMEM((rows, ff), jnp.bfloat16),
            pltpu.SemaphoreType.DMA((5 + len(hidden_parts(ff)),)),
        ],
        compiler_params=pltpu.CompilerParams(vmem_limit_bytes=28 * MIB + 8 * nodes * D),
        name="points",
    )(me, *in_hbm)


def nodes_kernel(devices, rows, me_ref, mine_ref, other_ref, out_ref, own_ref):
    def part(start, size):
        at = slice(start, start + size)
        return mine_ref[at, :].astype(jnp.float32) + other_ref[at, :].astype(jnp.float32)

    shift = digit_bits(devices)
    digits = -(-total_bits(rows) // shift)
    lane = lax.broadcasted_iota(jnp.int32, (TOTAL_ROWS, LANES), 1)
    digit = lane % LANES_PER_GROUP
    worth = jnp.where(digit < digits, 1 << jnp.minimum(digit * shift, 30), 0).astype(jnp.float32)
    tile = part(COLS * GROUP_ROWS, TOTAL_ROWS) * worth
    totals = jnp.concatenate(
        [
            jnp.sum(jnp.where(lane // LANES_PER_GROUP == g, tile, 0.0), axis=1, keepdims=True)
            for g in range(GROUP_ROWS // TOTAL_ROWS)
        ],
        axis=0,
    )
    pooled = jnp.concatenate(
        [part(col * GROUP_ROWS, GROUP_ROWS) for col in range(COLS)], axis=1
    ) / (1.0 + totals)
    scale = lax.rsqrt(jnp.mean(pooled * pooled, axis=-1, keepdims=True) + 1e-06)
    out_ref[...] = (pooled * scale).astype(jnp.bfloat16)
    first = me_ref[0] // (devices // 2) * S_DEV
    own_ref[...] = out_ref[pl.ds(pl.multiple_of(first, S_DEV), S_DEV), :]


def run_nodes(devices, rows, me, mine, other):
    return pl.pallas_call(
        functools.partial(nodes_kernel, devices, rows),
        in_specs=[pl.BlockSpec(memory_space=pltpu.SMEM)]
        + [pl.BlockSpec(memory_space=pltpu.VMEM)] * 2,
        out_shape=[
            pltpu.VMEM((GROUP_ROWS, D), jnp.bfloat16),
            pltpu.VMEM((S_DEV, D), jnp.bfloat16),
        ],
        compiler_params=pltpu.CompilerParams(vmem_limit_bytes=8 * MIB),
        name="nodes",
    )(me, *in_vmem(mine, other))


def in_vmem(*arrays):
    return [pltpu.with_memory_space_constraint(array, pltpu.VMEM) for array in arrays]


def project(rows, proj_ref, start, size):
    return jnp.dot(
        rows, proj_ref[:, start : start + size], preferred_element_type=jnp.float32
    ).astype(jnp.bfloat16)


def partial_kernel(own_ref, other_ref, proj_ref, *refs):
    *pieces, mine_ref, theirs_ref, nodes_ref = refs
    start = 0
    for piece in pieces:
        nodes_ref[start : start + piece.shape[0], :] = piece[...]
        start += piece.shape[0]
    queries = project(
        jnp.concatenate([own_ref[...], other_ref[...]], axis=0), proj_ref, 0, D
    )
    keys = project(nodes_ref[...], proj_ref, D, D)
    values = project(nodes_ref[...], proj_ref, 2 * D, D)
    rows = 2 * S_DEV
    lane = lax.broadcasted_iota(jnp.int32, (rows, LANES), 1)
    low = lane < DH
    stats = jnp.zeros((rows, LANES), jnp.float32)
    for pair in range(COLS):
        at = slice(pair * LANES, (pair + 1) * LANES)
        both = queries[:, at]
        zero = jnp.zeros_like(both)
        stacked = jnp.concatenate(
            [jnp.where(low, both, zero), jnp.where(low, zero, both)], axis=0
        )
        scores = lax.dot_general(
            stacked, keys[:, at], (((1,), (1,)), ((), ())), preferred_element_type=jnp.float32
        ) * (DH**-0.5)
        highest = jnp.max(scores, axis=-1, keepdims=True)
        exps = jnp.exp(scores - highest)
        total = jnp.sum(exps, axis=-1, keepdims=True)
        summed = jnp.dot(
            exps.astype(jnp.bfloat16), values[:, at], preferred_element_type=jnp.float32
        )
        for half in (0, 1):
            these = slice(half * rows, (half + 1) * rows)
            stats = jnp.where(lane == 2 * pair + half, highest[these], stats)
            stats = jnp.where(lane == DH + 2 * pair + half, total[these], stats)
        piece = jnp.where(low, summed[:rows], summed[rows:])
        mine_ref[:, at] = piece[:S_DEV]
        theirs_ref[:, at] = piece[S_DEV:]
    mine_ref[:, D:] = stats[:S_DEV]
    theirs_ref[:, D:] = stats[S_DEV:]


def run_partial(own, other, proj_weight, pieces):
    rows = sum(piece.shape[0] for piece in pieces)
    out = pltpu.VMEM((S_DEV, D + LANES), jnp.float32)
    return pl.pallas_call(
        partial_kernel,
        out_shape=[out, out],
        scratch_shapes=[pltpu.VMEM((rows, D), jnp.bfloat16)],
        compiler_params=pltpu.CompilerParams(vmem_limit_bytes=12 * MIB + 24 * rows * D),
        name="partial",
    )(*in_vmem(own, other, proj_weight, *pieces))


def merge_kernel(mine_ref, theirs_ref, gain_ref, out_ref):
    mine, theirs = mine_ref[:, D:], theirs_ref[:, D:]
    highest = jnp.maximum(mine, theirs)
    mine_scale, theirs_scale = jnp.exp(mine - highest), jnp.exp(theirs - highest)
    mine_total = pltpu.roll(mine, DH, 1)
    theirs_total = pltpu.roll(theirs, DH, 1)
    total = mine_total * mine_scale + theirs_total * theirs_scale
    mine_scale, theirs_scale = mine_scale / total, theirs_scale / total
    low = lax.broadcasted_iota(jnp.int32, (S_DEV, LANES), 1) < DH
    heads = []
    for pair in range(COLS):
        at = slice(pair * LANES, (pair + 1) * LANES)
        first, second = slice(2 * pair, 2 * pair + 1), slice(2 * pair + 1, 2 * pair + 2)
        heads.append(
            mine_ref[:, at] * jnp.where(low, mine_scale[:, first], mine_scale[:, second])
            + theirs_ref[:, at] * jnp.where(low, theirs_scale[:, first], theirs_scale[:, second])
        )
    attended = jnp.concatenate(heads, axis=1)
    scale = lax.rsqrt(jnp.mean(attended * attended, axis=-1, keepdims=True) + 1e-06)
    out_ref[...] = (attended * scale * gain_ref[...].astype(jnp.float32)).astype(jnp.bfloat16)


def run_merge(mine, theirs, gain):
    return pl.pallas_call(
        merge_kernel,
        out_shape=jax.ShapeDtypeStruct((S_DEV, D), jnp.bfloat16),
        compiler_params=pltpu.CompilerParams(vmem_limit_bytes=8 * MIB),
        name="merge",
    )(*in_vmem(mine, theirs), gain)


def add_up(first, *rest):
    total = first.astype(jnp.float32)
    for term in rest:
        total = total + term.astype(jnp.float32)
    return total.astype(jnp.bfloat16)


def body(
    points_in,
    hidden_weight,
    output_weight,
    point_owner,
    point_node,
    point_weight,
    proj_weight,
    final_gain,
):
    rows = points_in.shape[0]
    devices = lax.axis_size("blk")
    me = lax.axis_index("blk").astype(jnp.int32).reshape(1)

    def swap(array, flip):
        return lax.ppermute(array, "blk", [(i, i ^ flip) for i in range(devices)])

    send, keep = run_points(
        devices,
        me,
        points_in,
        hidden_weight,
        output_weight,
        point_owner.reshape(1, rows),
        point_node.reshape(1, rows),
        point_weight.reshape(1, rows),
    )
    table = add_up(keep, swap(send, 1))
    groups = []
    width = (devices // 4).bit_length() - 1
    while width > 0:
        take = min(2, width)
        width -= take
        groups.append((take, width))
    for take, width in groups:
        size = (1 << width) * CHUNK
        parts = [table[j * size : (j + 1) * size] for j in range(1 << take)]
        order = (2, 1, 3) if take == 2 else (1,)
        table = add_up(parts[0], *[swap(parts[j], j << (width + 1)) for j in order])
    nodes, own = run_nodes(devices, rows, me, table, swap(table, devices // 2))
    pieces = [nodes]
    for take, width in groups[::-1]:
        pieces += [
            swap(piece, j << (width + 1))
            for j in ((3, 1, 2) if take == 2 else (1,))
            for piece in pieces
        ]
    pieces[1], held = lax.optimization_barrier((pieces[1], own))
    other = swap(held, 1)
    mine, theirs = run_partial(own, other, proj_weight, pieces)
    return run_merge(mine, swap(theirs, 1), final_gain.reshape(1, D))


def solution(mesh):
    placed = (
        P(("groups", "blk"), None),
        P(),
        P(),
        P(("groups", "blk"), None),
        P(("groups", "blk")),
        P(("groups", "blk")),
        P(),
        P(),
    )
    return jax.shard_map(
        body, mesh=mesh, in_specs=placed, out_specs=P(("groups", "blk"), None), check_vma=False
    )
```

```python
import functools

import jax
import jax.numpy as jnp
from jax import lax
from jax.experimental import pallas as pl
from jax.experimental.pallas import tpu as pltpu
from jax.sharding import PartitionSpec as P

D = 768
HEADS = 12
S_DEV = 32
DH = 64
LANES = 128
GROUP_ROWS = 2 * S_DEV
COLS = D // LANES
TOTAL_ROWS = 16
CHUNK = COLS * GROUP_ROWS + TOTAL_ROWS
LANES_PER_GROUP = LANES // (GROUP_ROWS // TOTAL_ROWS)
MIB = 1024 * 1024


def digit_bits(devices):
    return max(1, (256 // devices).bit_length() - 1)


def total_bits(rows):
    return (4 * rows).bit_length()


def gelu(values):
    return 0.5 * values * (1.0 + lax.erf(values * 0.7071067811865476))


def hidden_parts(ff):
    stops = [stop for stop in (768,) if stop < ff] + [ff]
    return [slice(start, stop) for start, stop in zip([0] + stops[:-1], stops)]


def points_kernel(
    devices, me_ref, x_hbm, hidden_hbm, output_hbm, owner_hbm, node_hbm, weight_hbm,
    send_ref, keep_ref, owner_ref, node_ref, weight_ref, x_ref, normed_ref, hidden_ref, output_ref, coeffs_ref, middle_ref, sems,
):
    rows = x_ref.shape[0]
    ff = hidden_ref.shape[1]
    parts = hidden_parts(ff)

    def hidden_copy(part):
        at = parts[part]
        return pltpu.make_async_copy(hidden_hbm.at[:, at], hidden_ref.at[:, at], sems.at[2 + part])

    x_copy = pltpu.make_async_copy(x_hbm, x_ref, sems.at[0])
    output_copy = pltpu.make_async_copy(output_hbm, output_ref, sems.at[1])
    index_copies = [
        pltpu.make_async_copy(source, target, sems.at[2 + len(parts) + i])
        for i, (source, target) in enumerate(
            ((owner_hbm, owner_ref), (node_hbm, node_ref), (weight_hbm, weight_ref))
        )
    ]
    for copy in index_copies:
        copy.start()
    x_copy.start()
    for part in range(len(parts)):
        hidden_copy(part).start()
    output_copy.start()

    chunks = devices // 4
    half = chunks * GROUP_ROWS
    places = [
        (out_ref, chunk * CHUNK, core * half + chunk * GROUP_ROWS)
        for core, out_ref in ((0, keep_ref), (1, send_ref))
        for chunk in range(chunks)
    ]
    me = me_ref[0]

    @pl.when(me >= 0)
    def _():
        for copy in index_copies:
            copy.wait()
        owner = owner_ref[...]
        near = (owner ^ me) & (devices // 2 - 1)
        row_of = (near // 2) * GROUP_ROWS + (owner // (devices // 2)) * S_DEV + node_ref[...]
        row_of = row_of + (near & 1) * half
        coeffs = jnp.where(
            row_of == lax.broadcasted_iota(jnp.int32, (2 * half, rows), 0), weight_ref[...], 0
        ).astype(jnp.float32)
        coeffs_ref[...] = coeffs.astype(jnp.bfloat16)
        totals = jnp.sum(coeffs, axis=1, keepdims=True).astype(jnp.int32)
        shift = digit_bits(devices)
        digits = -(-total_bits(rows) // shift)
        lane = lax.broadcasted_iota(jnp.int32, (TOTAL_ROWS, LANES), 1)
        digit = lane % LANES_PER_GROUP
        held = jnp.where(digit < digits, digit * shift, 31)
        for out_ref, base, first in places:
            tile = jnp.zeros((TOTAL_ROWS, LANES), jnp.int32)
            for group in range(GROUP_ROWS // TOTAL_ROWS):
                start = first + group * TOTAL_ROWS
                value = jnp.broadcast_to(totals[start : start + TOTAL_ROWS], (TOTAL_ROWS, LANES))
                tile = jnp.where(lane // LANES_PER_GROUP == group, value, tile)
            tile = (tile >> held) & ((1 << shift) - 1)
            out_ref[base + COLS * GROUP_ROWS : base + CHUNK, :] = tile.astype(
                jnp.float32
            ).astype(jnp.bfloat16)

    x_copy.wait()
    x = x_ref[...].astype(jnp.float32)
    scale = lax.rsqrt(jnp.mean(x * x, axis=-1, keepdims=True) + 1e-06)
    normed_ref[...] = (x * scale).astype(jnp.bfloat16)

    def one_part(part):
        at = parts[part]

        @pl.when(me > -2 - part)
        def _():
            hidden_copy(part).wait()
            middle_ref[:, at] = gelu(
                jnp.dot(normed_ref[...], hidden_ref[:, at], preferred_element_type=jnp.float32)
            ).astype(jnp.bfloat16)

    for part in range(len(parts)):
        one_part(part)
    output_copy.wait()
    sums = None
    half_rows = rows // 2
    for at in (slice(0, half_rows), slice(half_rows, rows)):
        features = (
            x_ref[at, :].astype(jnp.float32)
            + jnp.dot(middle_ref[at, :], output_ref[...], preferred_element_type=jnp.float32)
        ).astype(jnp.bfloat16)
        term = jnp.dot(coeffs_ref[:, at], features, preferred_element_type=jnp.float32)
        sums = term if sums is None else sums + term
    sums = sums.astype(jnp.bfloat16)
    for out_ref, base, first in places:
        for col in range(COLS):
            out_ref[base + col * GROUP_ROWS : base + (col + 1) * GROUP_ROWS, :] = sums[
                first : first + GROUP_ROWS, col * LANES : (col + 1) * LANES
            ]


def run_points(devices, me, x, hidden_weight, output_weight, owner, node, weight):
    rows, ff = x.shape[0], hidden_weight.shape[1]
    nodes = devices * S_DEV
    out = pltpu.VMEM((devices // 4 * CHUNK, LANES), jnp.bfloat16)
    hbm = pl.BlockSpec(memory_space=pl.ANY)
    vmem = pl.BlockSpec(memory_space=pltpu.VMEM)
    in_hbm = [
        pltpu.with_memory_space_constraint(array, pltpu.HBM)
        for array in (x, hidden_weight, output_weight, owner, node, weight)
    ]
    return pl.pallas_call(
        functools.partial(points_kernel, devices),
        in_specs=[pl.BlockSpec(memory_space=pltpu.SMEM)] + [hbm] * 6,
        out_specs=[vmem, vmem],
        out_shape=[out, out],
        scratch_shapes=[
            pltpu.VMEM((1, rows), jnp.int32),
            pltpu.VMEM((1, rows), jnp.int32),
            pltpu.VMEM((1, rows), jnp.int32),
            pltpu.VMEM((rows, D), jnp.bfloat16),
            pltpu.VMEM((rows, D), jnp.bfloat16),
            pltpu.VMEM((D, ff), jnp.bfloat16),
            pltpu.VMEM((ff, D), jnp.bfloat16),
            pltpu.VMEM((nodes, rows), jnp.bfloat16),
            pltpu.VMEM((rows, ff), jnp.bfloat16),
            pltpu.SemaphoreType.DMA((5 + len(hidden_parts(ff)),)),
        ],
        compiler_params=pltpu.CompilerParams(vmem_limit_bytes=28 * MIB + 8 * nodes * D),
        name="points",
    )(me, *in_hbm)


def nodes_kernel(devices, rows, mine_ref, other_ref, out_ref):
    def part(start, size):
        at = slice(start, start + size)
        return mine_ref[at, :].astype(jnp.float32) + other_ref[at, :].astype(jnp.float32)

    shift = digit_bits(devices)
    digits = -(-total_bits(rows) // shift)
    lane = lax.broadcasted_iota(jnp.int32, (TOTAL_ROWS, LANES), 1)
    digit = lane % LANES_PER_GROUP
    worth = jnp.where(digit < digits, 1 << jnp.minimum(digit * shift, 30), 0).astype(jnp.float32)
    tile = part(COLS * GROUP_ROWS, TOTAL_ROWS) * worth
    totals = jnp.concatenate(
        [
            jnp.sum(jnp.where(lane // LANES_PER_GROUP == g, tile, 0.0), axis=1, keepdims=True)
            for g in range(GROUP_ROWS // TOTAL_ROWS)
        ],
        axis=0,
    )
    pooled = jnp.concatenate(
        [part(col * GROUP_ROWS, GROUP_ROWS) for col in range(COLS)], axis=1
    ) / (1.0 + totals)
    scale = lax.rsqrt(jnp.mean(pooled * pooled, axis=-1, keepdims=True) + 1e-06)
    out_ref[...] = (pooled * scale).astype(jnp.bfloat16)


def run_nodes(devices, rows, mine, other):
    return pl.pallas_call(
        functools.partial(nodes_kernel, devices, rows),
        out_shape=pltpu.VMEM((GROUP_ROWS, D), jnp.bfloat16),
        compiler_params=pltpu.CompilerParams(vmem_limit_bytes=8 * MIB),
        name="nodes",
    )(*in_vmem(mine, other))


def in_vmem(*arrays):
    return [pltpu.with_memory_space_constraint(array, pltpu.VMEM) for array in arrays]


def project(rows, proj_ref, start, size):
    return jnp.dot(
        rows, proj_ref[:, start : start + size], preferred_element_type=jnp.float32
    ).astype(jnp.bfloat16)


def own_kernel(devices, me_ref, nodes_ref, proj_ref, query_ref, key_value_ref):
    first = pl.multiple_of(me_ref[0] // (devices // 2) * S_DEV, S_DEV)
    query_ref[...] = project(nodes_ref[pl.ds(first, S_DEV), :], proj_ref, 0, D)
    key_value_ref[...] = project(nodes_ref[...], proj_ref, D, 2 * D)


def run_own(devices, me, nodes, proj_weight):
    return pl.pallas_call(
        functools.partial(own_kernel, devices),
        in_specs=[pl.BlockSpec(memory_space=pltpu.SMEM)]
        + [pl.BlockSpec(memory_space=pltpu.VMEM)] * 2,
        out_shape=[
            pltpu.VMEM((S_DEV, D), jnp.bfloat16),
            pltpu.VMEM((GROUP_ROWS, 2 * D), jnp.bfloat16),
        ],
        compiler_params=pltpu.CompilerParams(vmem_limit_bytes=12 * MIB),
        cost_estimate=pl.CostEstimate(
            flops=2 * (S_DEV + 2 * GROUP_ROWS) * D * D, bytes_accessed=6 * D * D, transcendentals=0
        ),
        name="own",
    )(me, *in_vmem(nodes, proj_weight))


def partial_kernel(own_ref, other_ref, own_key_value_ref, proj_ref, *refs):
    *pieces, mine_ref, theirs_ref, nodes_ref = refs
    start = 0
    for piece in pieces:
        nodes_ref[start : start + piece.shape[0], :] = piece[...]
        start += piece.shape[0]
    queries = jnp.concatenate([own_ref[...], other_ref[...]], axis=0)
    key_value = jnp.concatenate(
        [own_key_value_ref[...], project(nodes_ref[...], proj_ref, D, 2 * D)], axis=0
    )
    keys, values = key_value[:, :D], key_value[:, D:]
    rows = 2 * S_DEV
    lane = lax.broadcasted_iota(jnp.int32, (rows, LANES), 1)
    low = lane < DH
    stats = jnp.zeros((rows, LANES), jnp.float32)
    for pair in range(COLS):
        at = slice(pair * LANES, (pair + 1) * LANES)
        both = queries[:, at]
        zero = jnp.zeros_like(both)
        stacked = jnp.concatenate(
            [jnp.where(low, both, zero), jnp.where(low, zero, both)], axis=0
        )
        scores = lax.dot_general(
            stacked, keys[:, at], (((1,), (1,)), ((), ())), preferred_element_type=jnp.float32
        ) * (DH**-0.5)
        highest = jnp.max(scores, axis=-1, keepdims=True)
        exps = jnp.exp(scores - highest)
        total = jnp.sum(exps, axis=-1, keepdims=True)
        summed = jnp.dot(
            exps.astype(jnp.bfloat16), values[:, at], preferred_element_type=jnp.float32
        )
        for half in (0, 1):
            these = slice(half * rows, (half + 1) * rows)
            stats = jnp.where(lane == 2 * pair + half, highest[these], stats)
            stats = jnp.where(lane == DH + 2 * pair + half, total[these], stats)
        piece = jnp.where(low, summed[:rows], summed[rows:])
        mine_ref[:, at] = piece[:S_DEV]
        theirs_ref[:, at] = piece[S_DEV:]
    mine_ref[:, D:] = stats[:S_DEV]
    theirs_ref[:, D:] = stats[S_DEV:]


def run_partial(own, other, own_key_value, proj_weight, pieces):
    rows = sum(piece.shape[0] for piece in pieces)
    out = pltpu.VMEM((S_DEV, D + LANES), jnp.float32)
    return pl.pallas_call(
        partial_kernel,
        out_shape=[out, out],
        scratch_shapes=[pltpu.VMEM((rows, D), jnp.bfloat16)],
        compiler_params=pltpu.CompilerParams(vmem_limit_bytes=12 * MIB + 24 * rows * D),
        name="partial",
    )(*in_vmem(own, other, own_key_value, proj_weight, *pieces))


def merge_kernel(mine_ref, theirs_ref, gain_ref, out_ref):
    mine, theirs = mine_ref[:, D:], theirs_ref[:, D:]
    highest = jnp.maximum(mine, theirs)
    mine_scale, theirs_scale = jnp.exp(mine - highest), jnp.exp(theirs - highest)
    mine_total = pltpu.roll(mine, DH, 1)
    theirs_total = pltpu.roll(theirs, DH, 1)
    total = mine_total * mine_scale + theirs_total * theirs_scale
    mine_scale, theirs_scale = mine_scale / total, theirs_scale / total
    low = lax.broadcasted_iota(jnp.int32, (S_DEV, LANES), 1) < DH
    heads = []
    for pair in range(COLS):
        at = slice(pair * LANES, (pair + 1) * LANES)
        first, second = slice(2 * pair, 2 * pair + 1), slice(2 * pair + 1, 2 * pair + 2)
        heads.append(
            mine_ref[:, at] * jnp.where(low, mine_scale[:, first], mine_scale[:, second])
            + theirs_ref[:, at] * jnp.where(low, theirs_scale[:, first], theirs_scale[:, second])
        )
    attended = jnp.concatenate(heads, axis=1)
    scale = lax.rsqrt(jnp.mean(attended * attended, axis=-1, keepdims=True) + 1e-06)
    out_ref[...] = (attended * scale * gain_ref[...].astype(jnp.float32)).astype(jnp.bfloat16)


def run_merge(mine, theirs, gain):
    return pl.pallas_call(
        merge_kernel,
        out_shape=jax.ShapeDtypeStruct((S_DEV, D), jnp.bfloat16),
        compiler_params=pltpu.CompilerParams(vmem_limit_bytes=8 * MIB),
        name="merge",
    )(*in_vmem(mine, theirs), gain)


def add_up(first, *rest):
    total = first.astype(jnp.float32)
    for term in rest:
        total = total + term.astype(jnp.float32)
    return total.astype(jnp.bfloat16)


def body(
    points_in,
    hidden_weight,
    output_weight,
    point_owner,
    point_node,
    point_weight,
    proj_weight,
    final_gain,
):
    rows = points_in.shape[0]
    devices = lax.axis_size("blk")
    me = lax.axis_index("blk").astype(jnp.int32).reshape(1)

    def swap(array, flip):
        return lax.ppermute(array, "blk", [(i, i ^ flip) for i in range(devices)])

    send, keep = run_points(
        devices,
        me,
        points_in,
        hidden_weight,
        output_weight,
        point_owner.reshape(1, rows),
        point_node.reshape(1, rows),
        point_weight.reshape(1, rows),
    )
    table = add_up(keep, swap(send, 1))
    groups = []
    width = (devices // 4).bit_length() - 1
    while width > 0:
        take = min(2, width)
        width -= take
        groups.append((take, width))
    for take, width in groups:
        size = (1 << width) * CHUNK
        parts = [table[j * size : (j + 1) * size] for j in range(1 << take)]
        order = (2, 1, 3) if take == 2 else (1,)
        table = add_up(parts[0], *[swap(parts[j], j << (width + 1)) for j in order])
    nodes = run_nodes(devices, rows, table, swap(table, devices // 2))
    pieces = [nodes]
    for take, width in groups[::-1]:
        pieces += [
            swap(piece, j << (width + 1))
            for j in ((3, 1, 2) if take == 2 else (1,))
            for piece in pieces
        ]
    own, own_key_value = run_own(devices, me, nodes, proj_weight)
    mine, theirs = run_partial(own, swap(own, 1), own_key_value, proj_weight, pieces[1:])
    return run_merge(mine, swap(theirs, 1), final_gain.reshape(1, D))


def solution(mesh):
    placed = (
        P(("groups", "blk"), None),
        P(),
        P(),
        P(("groups", "blk"), None),
        P(("groups", "blk")),
        P(("groups", "blk")),
        P(),
        P(),
    )
    return jax.shard_map(
        body, mesh=mesh, in_specs=placed, out_specs=P(("groups", "blk"), None), check_vma=False
    )
```

```python
import functools

import jax
import jax.numpy as jnp
from jax import lax
from jax.experimental import pallas as pl
from jax.experimental.pallas import tpu as pltpu
from jax.sharding import PartitionSpec as P

D = 768
HEADS = 12
S_DEV = 32
DH = 64
LANES = 128
GROUP_ROWS = 2 * S_DEV
COLS = D // LANES
TOTAL_ROWS = 16
CHUNK = COLS * GROUP_ROWS + TOTAL_ROWS
LANES_PER_GROUP = LANES // (GROUP_ROWS // TOTAL_ROWS)
MIB = 1024 * 1024


def digit_bits(devices):
    return max(1, (256 // devices).bit_length() - 1)


def total_bits(rows):
    return (4 * rows).bit_length()


def gelu(values):
    return 0.5 * values * (1.0 + lax.erf(values * 0.7071067811865476))


def hidden_parts(ff):
    stops = [stop for stop in (768,) if stop < ff] + [ff]
    return [slice(start, stop) for start, stop in zip([0] + stops[:-1], stops)]


def points_kernel(
    devices, me_ref, x_hbm, hidden_hbm, output_hbm, owner_hbm, node_hbm, weight_hbm,
    send_ref, features_ref, kept_ref, tiles_ref, owner_ref, node_ref, weight_ref, x_ref, normed_ref, hidden_ref, output_ref, coeffs_ref, middle_ref, sems,
):
    rows = x_ref.shape[0]
    ff = hidden_ref.shape[1]
    parts = hidden_parts(ff)

    def hidden_copy(part):
        at = parts[part]
        return pltpu.make_async_copy(hidden_hbm.at[:, at], hidden_ref.at[:, at], sems.at[2 + part])

    x_copy = pltpu.make_async_copy(x_hbm, x_ref, sems.at[0])
    output_copy = pltpu.make_async_copy(output_hbm, output_ref, sems.at[1])
    index_copies = [
        pltpu.make_async_copy(source, target, sems.at[2 + len(parts) + i])
        for i, (source, target) in enumerate(
            ((owner_hbm, owner_ref), (node_hbm, node_ref), (weight_hbm, weight_ref))
        )
    ]
    for copy in index_copies:
        copy.start()
    x_copy.start()
    for part in range(len(parts)):
        hidden_copy(part).start()
    output_copy.start()

    chunks = devices // 4
    half = chunks * GROUP_ROWS
    me = me_ref[0]

    @pl.when(me >= 0)
    def _():
        for copy in index_copies:
            copy.wait()
        owner = owner_ref[...]
        near = (owner ^ me) & (devices // 2 - 1)
        row_of = (near // 2) * GROUP_ROWS + (owner // (devices // 2)) * S_DEV + node_ref[...]
        row_of = row_of + (near & 1) * half
        coeffs = jnp.where(
            row_of == lax.broadcasted_iota(jnp.int32, (2 * half, rows), 0), weight_ref[...], 0
        ).astype(jnp.float32)
        kept_ref[...] = coeffs[:half].astype(jnp.bfloat16)
        coeffs_ref[...] = coeffs[half:].astype(jnp.bfloat16)
        totals = jnp.sum(coeffs, axis=1, keepdims=True).astype(jnp.int32)
        shift = digit_bits(devices)
        digits = -(-total_bits(rows) // shift)
        lane = lax.broadcasted_iota(jnp.int32, (TOTAL_ROWS, LANES), 1)
        digit = lane % LANES_PER_GROUP
        held = jnp.where(digit < digits, digit * shift, 31)
        for chunk in range(2 * chunks):
            tile = jnp.zeros((TOTAL_ROWS, LANES), jnp.int32)
            for group in range(GROUP_ROWS // TOTAL_ROWS):
                start = chunk * GROUP_ROWS + group * TOTAL_ROWS
                value = jnp.broadcast_to(totals[start : start + TOTAL_ROWS], (TOTAL_ROWS, LANES))
                tile = jnp.where(lane // LANES_PER_GROUP == group, value, tile)
            tile = ((tile >> held) & ((1 << shift) - 1)).astype(jnp.float32).astype(jnp.bfloat16)
            if chunk < chunks:
                tiles_ref[chunk * TOTAL_ROWS : (chunk + 1) * TOTAL_ROWS, :] = tile
            else:
                end = (chunk - chunks + 1) * CHUNK
                send_ref[end - TOTAL_ROWS : end, :] = tile

    x_copy.wait()
    x = x_ref[...].astype(jnp.float32)
    scale = lax.rsqrt(jnp.mean(x * x, axis=-1, keepdims=True) + 1e-06)
    normed_ref[...] = (x * scale).astype(jnp.bfloat16)

    def one_part(part):
        at = parts[part]

        @pl.when(me > -2 - part)
        def _():
            hidden_copy(part).wait()
            middle_ref[:, at] = gelu(
                jnp.dot(normed_ref[...], hidden_ref[:, at], preferred_element_type=jnp.float32)
            ).astype(jnp.bfloat16)

    for part in range(len(parts)):
        one_part(part)
    output_copy.wait()
    sums = None
    half_rows = rows // 2
    for at in (slice(0, half_rows), slice(half_rows, rows)):
        features = (
            x_ref[at, :].astype(jnp.float32)
            + jnp.dot(middle_ref[at, :], output_ref[...], preferred_element_type=jnp.float32)
        ).astype(jnp.bfloat16)
        features_ref[at, :] = features
        term = jnp.dot(coeffs_ref[:, at], features, preferred_element_type=jnp.float32)
        sums = term if sums is None else sums + term
    store_table(send_ref, sums.astype(jnp.bfloat16))


def store_table(out_ref, sums):
    for first in range(0, sums.shape[0], GROUP_ROWS):
        for col in range(COLS):
            at = first // GROUP_ROWS * CHUNK + col * GROUP_ROWS
            out_ref[at : at + GROUP_ROWS, :] = sums[
                first : first + GROUP_ROWS, col * LANES : (col + 1) * LANES
            ]


def keep_kernel(features_ref, kept_ref, tiles_ref, out_ref):
    sums = jnp.dot(kept_ref[...], features_ref[...], preferred_element_type=jnp.float32)
    store_table(out_ref, sums.astype(jnp.bfloat16))
    for chunk in range(tiles_ref.shape[0] // TOTAL_ROWS):
        end = (chunk + 1) * CHUNK
        out_ref[end - TOTAL_ROWS : end, :] = tiles_ref[
            chunk * TOTAL_ROWS : (chunk + 1) * TOTAL_ROWS, :
        ]


def run_keep(features, kept, tiles):
    nodes, rows = kept.shape
    return pl.pallas_call(
        keep_kernel,
        out_shape=pltpu.VMEM((nodes // GROUP_ROWS * CHUNK, LANES), jnp.bfloat16),
        compiler_params=pltpu.CompilerParams(vmem_limit_bytes=8 * MIB + 16 * nodes * D),
        cost_estimate=pl.CostEstimate(
            flops=2 * nodes * rows * D, bytes_accessed=4 * nodes * D, transcendentals=0
        ),
        name="keep",
    )(*in_vmem(features, kept, tiles))


def run_points(devices, me, x, hidden_weight, output_weight, owner, node, weight):
    rows, ff = x.shape[0], hidden_weight.shape[1]
    nodes = devices * S_DEV
    out = pltpu.VMEM((devices // 4 * CHUNK, LANES), jnp.bfloat16)
    hbm = pl.BlockSpec(memory_space=pl.ANY)
    vmem = pl.BlockSpec(memory_space=pltpu.VMEM)
    in_hbm = [
        pltpu.with_memory_space_constraint(array, pltpu.HBM)
        for array in (x, hidden_weight, output_weight, owner, node, weight)
    ]
    return pl.pallas_call(
        functools.partial(points_kernel, devices),
        in_specs=[pl.BlockSpec(memory_space=pltpu.SMEM)] + [hbm] * 6,
        out_specs=[vmem] * 4,
        out_shape=[
            out,
            pltpu.VMEM((rows, D), jnp.bfloat16),
            pltpu.VMEM((nodes // 2, rows), jnp.bfloat16),
            pltpu.VMEM((devices // 4 * TOTAL_ROWS, LANES), jnp.bfloat16),
        ],
        scratch_shapes=[
            pltpu.VMEM((1, rows), jnp.int32),
            pltpu.VMEM((1, rows), jnp.int32),
            pltpu.VMEM((1, rows), jnp.int32),
            pltpu.VMEM((rows, D), jnp.bfloat16),
            pltpu.VMEM((rows, D), jnp.bfloat16),
            pltpu.VMEM((D, ff), jnp.bfloat16),
            pltpu.VMEM((ff, D), jnp.bfloat16),
            pltpu.VMEM((nodes // 2, rows), jnp.bfloat16),
            pltpu.VMEM((rows, ff), jnp.bfloat16),
            pltpu.SemaphoreType.DMA((5 + len(hidden_parts(ff)),)),
        ],
        compiler_params=pltpu.CompilerParams(vmem_limit_bytes=28 * MIB + 8 * nodes * D),
        name="points",
    )(me, *in_hbm)


def nodes_kernel(devices, rows, mine_ref, other_ref, out_ref):
    def part(start, size):
        at = slice(start, start + size)
        return mine_ref[at, :].astype(jnp.float32) + other_ref[at, :].astype(jnp.float32)

    shift = digit_bits(devices)
    digits = -(-total_bits(rows) // shift)
    lane = lax.broadcasted_iota(jnp.int32, (TOTAL_ROWS, LANES), 1)
    digit = lane % LANES_PER_GROUP
    worth = jnp.where(digit < digits, 1 << jnp.minimum(digit * shift, 30), 0).astype(jnp.float32)
    tile = part(COLS * GROUP_ROWS, TOTAL_ROWS) * worth
    totals = jnp.concatenate(
        [
            jnp.sum(jnp.where(lane // LANES_PER_GROUP == g, tile, 0.0), axis=1, keepdims=True)
            for g in range(GROUP_ROWS // TOTAL_ROWS)
        ],
        axis=0,
    )
    pooled = jnp.concatenate(
        [part(col * GROUP_ROWS, GROUP_ROWS) for col in range(COLS)], axis=1
    ) / (1.0 + totals)
    scale = lax.rsqrt(jnp.mean(pooled * pooled, axis=-1, keepdims=True) + 1e-06)
    out_ref[...] = (pooled * scale).astype(jnp.bfloat16)


def run_nodes(devices, rows, mine, other):
    return pl.pallas_call(
        functools.partial(nodes_kernel, devices, rows),
        out_shape=pltpu.VMEM((GROUP_ROWS, D), jnp.bfloat16),
        compiler_params=pltpu.CompilerParams(vmem_limit_bytes=8 * MIB),
        name="nodes",
    )(*in_vmem(mine, other))


def in_vmem(*arrays):
    return [pltpu.with_memory_space_constraint(array, pltpu.VMEM) for array in arrays]


def project(rows, proj_ref, start, size):
    return jnp.dot(
        rows, proj_ref[:, start : start + size], preferred_element_type=jnp.float32
    ).astype(jnp.bfloat16)


def own_kernel(devices, me_ref, nodes_ref, proj_ref, query_ref, key_value_ref):
    first = pl.multiple_of(me_ref[0] // (devices // 2) * S_DEV, S_DEV)
    query_ref[...] = project(nodes_ref[pl.ds(first, S_DEV), :], proj_ref, 0, D)
    key_value_ref[...] = project(nodes_ref[...], proj_ref, D, 2 * D)


def run_own(devices, me, nodes, proj_weight):
    return pl.pallas_call(
        functools.partial(own_kernel, devices),
        in_specs=[pl.BlockSpec(memory_space=pltpu.SMEM)]
        + [pl.BlockSpec(memory_space=pltpu.VMEM)] * 2,
        out_shape=[
            pltpu.VMEM((S_DEV, D), jnp.bfloat16),
            pltpu.VMEM((GROUP_ROWS, 2 * D), jnp.bfloat16),
        ],
        compiler_params=pltpu.CompilerParams(vmem_limit_bytes=12 * MIB),
        cost_estimate=pl.CostEstimate(
            flops=2 * (S_DEV + 2 * GROUP_ROWS) * D * D, bytes_accessed=6 * D * D, transcendentals=0
        ),
        name="own",
    )(me, *in_vmem(nodes, proj_weight))


def partial_kernel(own_ref, other_ref, own_key_value_ref, proj_ref, *refs):
    *pieces, mine_ref, theirs_ref, nodes_ref = refs
    start = 0
    for piece in pieces:
        nodes_ref[start : start + piece.shape[0], :] = piece[...]
        start += piece.shape[0]
    queries = jnp.concatenate([own_ref[...], other_ref[...]], axis=0)
    key_value = jnp.concatenate(
        [own_key_value_ref[...], project(nodes_ref[...], proj_ref, D, 2 * D)], axis=0
    )
    keys, values = key_value[:, :D], key_value[:, D:]
    rows = 2 * S_DEV
    lane = lax.broadcasted_iota(jnp.int32, (rows, LANES), 1)
    low = lane < DH
    stats = jnp.zeros((rows, LANES), jnp.float32)
    for pair in range(COLS):
        at = slice(pair * LANES, (pair + 1) * LANES)
        both = queries[:, at]
        zero = jnp.zeros_like(both)
        stacked = jnp.concatenate(
            [jnp.where(low, both, zero), jnp.where(low, zero, both)], axis=0
        )
        scores = lax.dot_general(
            stacked, keys[:, at], (((1,), (1,)), ((), ())), preferred_element_type=jnp.float32
        ) * (DH**-0.5)
        highest = jnp.max(scores, axis=-1, keepdims=True)
        exps = jnp.exp(scores - highest)
        total = jnp.sum(exps, axis=-1, keepdims=True)
        summed = jnp.dot(
            exps.astype(jnp.bfloat16), values[:, at], preferred_element_type=jnp.float32
        )
        for half in (0, 1):
            these = slice(half * rows, (half + 1) * rows)
            stats = jnp.where(lane == 2 * pair + half, highest[these], stats)
            stats = jnp.where(lane == DH + 2 * pair + half, total[these], stats)
        piece = jnp.where(low, summed[:rows], summed[rows:])
        mine_ref[:, at] = piece[:S_DEV]
        theirs_ref[:, at] = piece[S_DEV:]
    mine_ref[:, D:] = stats[:S_DEV]
    theirs_ref[:, D:] = stats[S_DEV:]


def run_partial(own, other, own_key_value, proj_weight, pieces):
    rows = sum(piece.shape[0] for piece in pieces)
    out = pltpu.VMEM((S_DEV, D + LANES), jnp.float32)
    return pl.pallas_call(
        partial_kernel,
        out_shape=[out, out],
        scratch_shapes=[pltpu.VMEM((rows, D), jnp.bfloat16)],
        compiler_params=pltpu.CompilerParams(vmem_limit_bytes=12 * MIB + 24 * rows * D),
        name="partial",
    )(*in_vmem(own, other, own_key_value, proj_weight, *pieces))


def merge_kernel(mine_ref, theirs_ref, gain_ref, out_ref):
    mine, theirs = mine_ref[:, D:], theirs_ref[:, D:]
    highest = jnp.maximum(mine, theirs)
    mine_scale, theirs_scale = jnp.exp(mine - highest), jnp.exp(theirs - highest)
    mine_total = pltpu.roll(mine, DH, 1)
    theirs_total = pltpu.roll(theirs, DH, 1)
    total = mine_total * mine_scale + theirs_total * theirs_scale
    mine_scale, theirs_scale = mine_scale / total, theirs_scale / total
    low = lax.broadcasted_iota(jnp.int32, (S_DEV, LANES), 1) < DH
    heads = []
    for pair in range(COLS):
        at = slice(pair * LANES, (pair + 1) * LANES)
        first, second = slice(2 * pair, 2 * pair + 1), slice(2 * pair + 1, 2 * pair + 2)
        heads.append(
            mine_ref[:, at] * jnp.where(low, mine_scale[:, first], mine_scale[:, second])
            + theirs_ref[:, at] * jnp.where(low, theirs_scale[:, first], theirs_scale[:, second])
        )
    attended = jnp.concatenate(heads, axis=1)
    scale = lax.rsqrt(jnp.mean(attended * attended, axis=-1, keepdims=True) + 1e-06)
    out_ref[...] = (attended * scale * gain_ref[...].astype(jnp.float32)).astype(jnp.bfloat16)


def run_merge(mine, theirs, gain):
    return pl.pallas_call(
        merge_kernel,
        out_shape=jax.ShapeDtypeStruct((S_DEV, D), jnp.bfloat16),
        compiler_params=pltpu.CompilerParams(vmem_limit_bytes=8 * MIB),
        name="merge",
    )(*in_vmem(mine, theirs), gain)


def add_up(first, *rest):
    total = first.astype(jnp.float32)
    for term in rest:
        total = total + term.astype(jnp.float32)
    return total.astype(jnp.bfloat16)


def body(
    points_in,
    hidden_weight,
    output_weight,
    point_owner,
    point_node,
    point_weight,
    proj_weight,
    final_gain,
):
    rows = points_in.shape[0]
    devices = lax.axis_size("blk")
    me = lax.axis_index("blk").astype(jnp.int32).reshape(1)

    def swap(array, flip):
        return lax.ppermute(array, "blk", [(i, i ^ flip) for i in range(devices)])

    send, *kept = run_points(
        devices,
        me,
        points_in,
        hidden_weight,
        output_weight,
        point_owner.reshape(1, rows),
        point_node.reshape(1, rows),
        point_weight.reshape(1, rows),
    )
    table = add_up(run_keep(*kept), swap(send, 1))
    groups = []
    width = (devices // 4).bit_length() - 1
    while width > 0:
        take = min(2, width)
        width -= take
        groups.append((take, width))
    for take, width in groups:
        size = (1 << width) * CHUNK
        parts = [table[j * size : (j + 1) * size] for j in range(1 << take)]
        order = (2, 1, 3) if take == 2 else (1,)
        table = add_up(parts[0], *[swap(parts[j], j << (width + 1)) for j in order])
    nodes = run_nodes(devices, rows, table, swap(table, devices // 2))
    pieces = [nodes]
    for take, width in groups[::-1]:
        pieces += [
            swap(piece, j << (width + 1))
            for j in ((3, 1, 2) if take == 2 else (1,))
            for piece in pieces
        ]
    own, own_key_value = run_own(devices, me, nodes, proj_weight)
    mine, theirs = run_partial(own, swap(own, 1), own_key_value, proj_weight, pieces[1:])
    return run_merge(mine, swap(theirs, 1), final_gain.reshape(1, D))


def solution(mesh):
    placed = (
        P(("groups", "blk"), None),
        P(),
        P(),
        P(("groups", "blk"), None),
        P(("groups", "blk")),
        P(("groups", "blk")),
        P(),
        P(),
    )
    return jax.shard_map(
        body, mesh=mesh, in_specs=placed, out_specs=P(("groups", "blk"), None), check_vma=False
    )
```

```python
import functools

import jax
import jax.numpy as jnp
from jax import lax
from jax.experimental import pallas as pl
from jax.experimental.pallas import tpu as pltpu
from jax.sharding import PartitionSpec as P

D = 768
HEADS = 12
S_DEV = 32
DH = 64
LANES = 128
GROUP_ROWS = 2 * S_DEV
COLS = D // LANES
TOTAL_ROWS = 16
CHUNK = COLS * GROUP_ROWS + TOTAL_ROWS
LANES_PER_GROUP = LANES // (GROUP_ROWS // TOTAL_ROWS)
MIB = 1024 * 1024


def digit_bits(devices):
    return max(1, (256 // devices).bit_length() - 1)


def total_bits(rows):
    return (4 * rows).bit_length()


def gelu(values):
    return 0.5 * values * (1.0 + lax.erf(values * 0.7071067811865476))


def hidden_parts(ff):
    stops = [stop for stop in (768,) if stop < ff] + [ff]
    return [slice(start, stop) for start, stop in zip([0] + stops[:-1], stops)]


def points_kernel(
    devices, me_ref, x_hbm, hidden_hbm, output_hbm, owner_hbm, node_hbm, weight_hbm,
    own_ref, rest_ref, features_ref, kept_ref, tiles_ref, owner_ref, node_ref, weight_ref,
    x_ref, normed_ref, hidden_ref, output_ref, coeffs_ref, middle_ref, sems,
):
    rows = x_ref.shape[0]
    ff = hidden_ref.shape[1]
    parts = hidden_parts(ff)

    def hidden_copy(part):
        at = parts[part]
        return pltpu.make_async_copy(hidden_hbm.at[:, at], hidden_ref.at[:, at], sems.at[2 + part])

    x_copy = pltpu.make_async_copy(x_hbm, x_ref, sems.at[0])
    output_copy = pltpu.make_async_copy(output_hbm, output_ref, sems.at[1])
    index_copies = [
        pltpu.make_async_copy(source, target, sems.at[2 + len(parts) + i])
        for i, (source, target) in enumerate(
            ((owner_hbm, owner_ref), (node_hbm, node_ref), (weight_hbm, weight_ref))
        )
    ]
    for copy in index_copies:
        copy.start()
    x_copy.start()
    for part in range(len(parts)):
        hidden_copy(part).start()
    output_copy.start()

    chunks = devices // 4
    half = chunks * GROUP_ROWS
    me = me_ref[0]

    @pl.when(me >= 0)
    def _():
        for copy in index_copies:
            copy.wait()
        owner = owner_ref[...]
        near = (owner ^ me) & (devices // 2 - 1)
        row_of = (near // 2) * GROUP_ROWS + (owner // (devices // 2)) * S_DEV + node_ref[...]
        row_of = row_of + (near & 1) * half
        coeffs = jnp.where(
            row_of == lax.broadcasted_iota(jnp.int32, (2 * half, rows), 0), weight_ref[...], 0
        ).astype(jnp.float32)
        kept_ref[...] = coeffs[:half].astype(jnp.bfloat16)
        coeffs_ref[...] = coeffs[half:].astype(jnp.bfloat16)
        totals = jnp.sum(coeffs, axis=1, keepdims=True).astype(jnp.int32)
        shift = digit_bits(devices)
        digits = -(-total_bits(rows) // shift)
        lane = lax.broadcasted_iota(jnp.int32, (TOTAL_ROWS, LANES), 1)
        digit = lane % LANES_PER_GROUP
        held = jnp.where(digit < digits, digit * shift, 31)
        for chunk in range(2 * chunks):
            tile = jnp.zeros((TOTAL_ROWS, LANES), jnp.int32)
            for group in range(GROUP_ROWS // TOTAL_ROWS):
                start = chunk * GROUP_ROWS + group * TOTAL_ROWS
                value = jnp.broadcast_to(totals[start : start + TOTAL_ROWS], (TOTAL_ROWS, LANES))
                tile = jnp.where(lane // LANES_PER_GROUP == group, value, tile)
            tile = ((tile >> held) & ((1 << shift) - 1)).astype(jnp.float32).astype(jnp.bfloat16)
            if chunk < chunks:
                tiles_ref[chunk * TOTAL_ROWS : (chunk + 1) * TOTAL_ROWS, :] = tile
            else:
                store_totals(own_ref, rest_ref, chunk - chunks, tile)

    x_copy.wait()
    x = x_ref[...].astype(jnp.float32)
    scale = lax.rsqrt(jnp.mean(x * x, axis=-1, keepdims=True) + 1e-06)
    normed_ref[...] = (x * scale).astype(jnp.bfloat16)

    def one_part(part):
        at = parts[part]

        @pl.when(me > -2 - part)
        def _():
            hidden_copy(part).wait()
            middle_ref[:, at] = gelu(
                jnp.dot(normed_ref[...], hidden_ref[:, at], preferred_element_type=jnp.float32)
            ).astype(jnp.bfloat16)

    for part in range(len(parts)):
        one_part(part)
    output_copy.wait()
    sums = None
    half_rows = rows // 2
    for at in (slice(0, half_rows), slice(half_rows, rows)):
        features = (
            x_ref[at, :].astype(jnp.float32)
            + jnp.dot(middle_ref[at, :], output_ref[...], preferred_element_type=jnp.float32)
        ).astype(jnp.bfloat16)
        features_ref[at, :] = features
        term = jnp.dot(coeffs_ref[:, at], features, preferred_element_type=jnp.float32)
        sums = term if sums is None else sums + term
    sums = sums.astype(jnp.bfloat16)
    own_rows = own_ref.shape[0] // CHUNK * GROUP_ROWS
    store_table(own_ref, sums[:own_rows])
    store_table(rest_ref, sums[own_rows:])


def store_totals(own_ref, rest_ref, chunk, tile):
    own_chunks = own_ref.shape[0] // CHUNK
    out_ref, place = (own_ref, chunk) if chunk < own_chunks else (rest_ref, chunk - own_chunks)
    end = (place + 1) * CHUNK
    out_ref[end - TOTAL_ROWS : end, :] = tile


def store_table(out_ref, sums):
    for first in range(0, sums.shape[0], GROUP_ROWS):
        for col in range(COLS):
            at = first // GROUP_ROWS * CHUNK + col * GROUP_ROWS
            out_ref[at : at + GROUP_ROWS, :] = sums[
                first : first + GROUP_ROWS, col * LANES : (col + 1) * LANES
            ]


def keep_kernel(features_ref, kept_ref, tiles_ref, own_ref, rest_ref):
    sums = jnp.dot(kept_ref[...], features_ref[...], preferred_element_type=jnp.float32)
    sums = sums.astype(jnp.bfloat16)
    own_rows = own_ref.shape[0] // CHUNK * GROUP_ROWS
    store_table(own_ref, sums[:own_rows])
    store_table(rest_ref, sums[own_rows:])
    for chunk in range(tiles_ref.shape[0] // TOTAL_ROWS):
        tile = tiles_ref[chunk * TOTAL_ROWS : (chunk + 1) * TOTAL_ROWS, :]
        store_totals(own_ref, rest_ref, chunk, tile)


def run_keep(own_chunks, features, kept, tiles):
    nodes, rows = kept.shape
    rest_chunks = nodes // GROUP_ROWS - own_chunks
    return pl.pallas_call(
        keep_kernel,
        out_shape=[
            pltpu.VMEM((own_chunks * CHUNK, LANES), jnp.bfloat16),
            pltpu.VMEM((rest_chunks * CHUNK, LANES), jnp.bfloat16),
        ],
        compiler_params=pltpu.CompilerParams(vmem_limit_bytes=8 * MIB + 16 * nodes * D),
        cost_estimate=pl.CostEstimate(
            flops=2 * nodes * rows * D, bytes_accessed=4 * nodes * D, transcendentals=0
        ),
        name="keep",
    )(*in_vmem(features, kept, tiles))


def run_points(devices, own_chunks, me, x, hidden_weight, output_weight, owner, node, weight):
    rows, ff = x.shape[0], hidden_weight.shape[1]
    nodes = devices * S_DEV
    rest_chunks = devices // 4 - own_chunks
    hbm = pl.BlockSpec(memory_space=pl.ANY)
    vmem = pl.BlockSpec(memory_space=pltpu.VMEM)
    in_hbm = [
        pltpu.with_memory_space_constraint(array, pltpu.HBM)
        for array in (x, hidden_weight, output_weight, owner, node, weight)
    ]
    return pl.pallas_call(
        functools.partial(points_kernel, devices),
        in_specs=[pl.BlockSpec(memory_space=pltpu.SMEM)] + [hbm] * 6,
        out_specs=[vmem] * 5,
        out_shape=[
            pltpu.VMEM((own_chunks * CHUNK, LANES), jnp.bfloat16),
            pltpu.VMEM((rest_chunks * CHUNK, LANES), jnp.bfloat16),
            pltpu.VMEM((rows, D), jnp.bfloat16),
            pltpu.VMEM((nodes // 2, rows), jnp.bfloat16),
            pltpu.VMEM((devices // 4 * TOTAL_ROWS, LANES), jnp.bfloat16),
        ],
        scratch_shapes=[
            pltpu.VMEM((1, rows), jnp.int32),
            pltpu.VMEM((1, rows), jnp.int32),
            pltpu.VMEM((1, rows), jnp.int32),
            pltpu.VMEM((rows, D), jnp.bfloat16),
            pltpu.VMEM((rows, D), jnp.bfloat16),
            pltpu.VMEM((D, ff), jnp.bfloat16),
            pltpu.VMEM((ff, D), jnp.bfloat16),
            pltpu.VMEM((nodes // 2, rows), jnp.bfloat16),
            pltpu.VMEM((rows, ff), jnp.bfloat16),
            pltpu.SemaphoreType.DMA((5 + len(hidden_parts(ff)),)),
        ],
        compiler_params=pltpu.CompilerParams(vmem_limit_bytes=28 * MIB + 8 * nodes * D),
        name="points",
    )(me, *in_hbm)


def nodes_kernel(devices, rows, mine_ref, other_ref, out_ref):
    def part(start, size):
        at = slice(start, start + size)
        return mine_ref[at, :].astype(jnp.float32) + other_ref[at, :].astype(jnp.float32)

    shift = digit_bits(devices)
    digits = -(-total_bits(rows) // shift)
    lane = lax.broadcasted_iota(jnp.int32, (TOTAL_ROWS, LANES), 1)
    digit = lane % LANES_PER_GROUP
    worth = jnp.where(digit < digits, 1 << jnp.minimum(digit * shift, 30), 0).astype(jnp.float32)
    tile = part(COLS * GROUP_ROWS, TOTAL_ROWS) * worth
    totals = jnp.concatenate(
        [
            jnp.sum(jnp.where(lane // LANES_PER_GROUP == g, tile, 0.0), axis=1, keepdims=True)
            for g in range(GROUP_ROWS // TOTAL_ROWS)
        ],
        axis=0,
    )
    pooled = jnp.concatenate(
        [part(col * GROUP_ROWS, GROUP_ROWS) for col in range(COLS)], axis=1
    ) / (1.0 + totals)
    scale = lax.rsqrt(jnp.mean(pooled * pooled, axis=-1, keepdims=True) + 1e-06)
    out_ref[...] = (pooled * scale).astype(jnp.bfloat16)


def run_nodes(devices, rows, mine, other):
    return pl.pallas_call(
        functools.partial(nodes_kernel, devices, rows),
        out_shape=pltpu.VMEM((GROUP_ROWS, D), jnp.bfloat16),
        compiler_params=pltpu.CompilerParams(vmem_limit_bytes=8 * MIB),
        name="nodes",
    )(*in_vmem(mine, other))


def in_vmem(*arrays):
    return [pltpu.with_memory_space_constraint(array, pltpu.VMEM) for array in arrays]


def project(rows, proj_ref, start, size):
    return jnp.dot(
        rows, proj_ref[:, start : start + size], preferred_element_type=jnp.float32
    ).astype(jnp.bfloat16)


def own_kernel(devices, me_ref, nodes_ref, proj_ref, query_ref, key_value_ref):
    first = pl.multiple_of(me_ref[0] // (devices // 2) * S_DEV, S_DEV)
    query_ref[...] = project(nodes_ref[pl.ds(first, S_DEV), :], proj_ref, 0, D)
    key_value_ref[...] = project(nodes_ref[...], proj_ref, D, 2 * D)


def run_own(devices, me, nodes, proj_weight):
    return pl.pallas_call(
        functools.partial(own_kernel, devices),
        in_specs=[pl.BlockSpec(memory_space=pltpu.SMEM)]
        + [pl.BlockSpec(memory_space=pltpu.VMEM)] * 2,
        out_shape=[
            pltpu.VMEM((S_DEV, D), jnp.bfloat16),
            pltpu.VMEM((GROUP_ROWS, 2 * D), jnp.bfloat16),
        ],
        compiler_params=pltpu.CompilerParams(vmem_limit_bytes=12 * MIB),
        cost_estimate=pl.CostEstimate(
            flops=2 * (S_DEV + 2 * GROUP_ROWS) * D * D, bytes_accessed=6 * D * D, transcendentals=0
        ),
        name="own",
    )(me, *in_vmem(nodes, proj_weight))


def partial_kernel(own_ref, other_ref, own_key_value_ref, proj_ref, *refs):
    *pieces, mine_ref, theirs_ref, nodes_ref = refs
    start = 0
    for piece in pieces:
        nodes_ref[start : start + piece.shape[0], :] = piece[...]
        start += piece.shape[0]
    queries = jnp.concatenate([own_ref[...], other_ref[...]], axis=0)
    key_value = jnp.concatenate(
        [own_key_value_ref[...], project(nodes_ref[...], proj_ref, D, 2 * D)], axis=0
    )
    keys, values = key_value[:, :D], key_value[:, D:]
    rows = 2 * S_DEV
    lane = lax.broadcasted_iota(jnp.int32, (rows, LANES), 1)
    low = lane < DH
    stats = jnp.zeros((rows, LANES), jnp.float32)
    for pair in range(COLS):
        at = slice(pair * LANES, (pair + 1) * LANES)
        both = queries[:, at]
        zero = jnp.zeros_like(both)
        stacked = jnp.concatenate(
            [jnp.where(low, both, zero), jnp.where(low, zero, both)], axis=0
        )
        scores = lax.dot_general(
            stacked, keys[:, at], (((1,), (1,)), ((), ())), preferred_element_type=jnp.float32
        ) * (DH**-0.5)
        highest = jnp.max(scores, axis=-1, keepdims=True)
        exps = jnp.exp(scores - highest)
        total = jnp.sum(exps, axis=-1, keepdims=True)
        summed = jnp.dot(
            exps.astype(jnp.bfloat16), values[:, at], preferred_element_type=jnp.float32
        )
        for half in (0, 1):
            these = slice(half * rows, (half + 1) * rows)
            stats = jnp.where(lane == 2 * pair + half, highest[these], stats)
            stats = jnp.where(lane == DH + 2 * pair + half, total[these], stats)
        piece = jnp.where(low, summed[:rows], summed[rows:])
        mine_ref[:, at] = piece[:S_DEV]
        theirs_ref[:, at] = piece[S_DEV:]
    mine_ref[:, D:] = stats[:S_DEV]
    theirs_ref[:, D:] = stats[S_DEV:]


def run_partial(own, other, own_key_value, proj_weight, pieces):
    rows = sum(piece.shape[0] for piece in pieces)
    out = pltpu.VMEM((S_DEV, D + LANES), jnp.float32)
    return pl.pallas_call(
        partial_kernel,
        out_shape=[out, out],
        scratch_shapes=[pltpu.VMEM((rows, D), jnp.bfloat16)],
        compiler_params=pltpu.CompilerParams(vmem_limit_bytes=12 * MIB + 24 * rows * D),
        name="partial",
    )(*in_vmem(own, other, own_key_value, proj_weight, *pieces))


def merge_kernel(mine_ref, theirs_ref, gain_ref, out_ref):
    mine, theirs = mine_ref[:, D:], theirs_ref[:, D:]
    highest = jnp.maximum(mine, theirs)
    mine_scale, theirs_scale = jnp.exp(mine - highest), jnp.exp(theirs - highest)
    mine_total = pltpu.roll(mine, DH, 1)
    theirs_total = pltpu.roll(theirs, DH, 1)
    total = mine_total * mine_scale + theirs_total * theirs_scale
    mine_scale, theirs_scale = mine_scale / total, theirs_scale / total
    low = lax.broadcasted_iota(jnp.int32, (S_DEV, LANES), 1) < DH
    heads = []
    for pair in range(COLS):
        at = slice(pair * LANES, (pair + 1) * LANES)
        first, second = slice(2 * pair, 2 * pair + 1), slice(2 * pair + 1, 2 * pair + 2)
        heads.append(
            mine_ref[:, at] * jnp.where(low, mine_scale[:, first], mine_scale[:, second])
            + theirs_ref[:, at] * jnp.where(low, theirs_scale[:, first], theirs_scale[:, second])
        )
    attended = jnp.concatenate(heads, axis=1)
    scale = lax.rsqrt(jnp.mean(attended * attended, axis=-1, keepdims=True) + 1e-06)
    out_ref[...] = (attended * scale * gain_ref[...].astype(jnp.float32)).astype(jnp.bfloat16)


def run_merge(mine, theirs, gain):
    return pl.pallas_call(
        merge_kernel,
        out_shape=jax.ShapeDtypeStruct((S_DEV, D), jnp.bfloat16),
        compiler_params=pltpu.CompilerParams(vmem_limit_bytes=8 * MIB),
        name="merge",
    )(*in_vmem(mine, theirs), gain)


def add_up(first, *rest):
    total = first.astype(jnp.float32)
    for term in rest:
        total = total + term.astype(jnp.float32)
    return total.astype(jnp.bfloat16)


def body(
    points_in,
    hidden_weight,
    output_weight,
    point_owner,
    point_node,
    point_weight,
    proj_weight,
    final_gain,
):
    rows = points_in.shape[0]
    devices = lax.axis_size("blk")
    me = lax.axis_index("blk").astype(jnp.int32).reshape(1)

    def swap(array, flip):
        return lax.ppermute(array, "blk", [(i, i ^ flip) for i in range(devices)])

    groups = []
    width = (devices // 4).bit_length() - 1
    while width > 0:
        take = min(2, width)
        width -= take
        groups.append((take, width))
    own_chunks = 1 << groups[0][1]
    own_send, rest_send, *kept = run_points(
        devices,
        own_chunks,
        me,
        points_in,
        hidden_weight,
        output_weight,
        point_owner.reshape(1, rows),
        point_node.reshape(1, rows),
        point_weight.reshape(1, rows),
    )
    rest_got = swap(rest_send, 1)
    own_got = swap(own_send, 1)
    own_kept, rest_kept = run_keep(own_chunks, *kept)
    sent = add_up(rest_kept, rest_got)
    terms = [own_kept, own_got]
    for take, width in groups:
        size = (1 << width) * CHUNK
        order = (2, 1, 3) if take == 2 else (1,)
        table = add_up(
            *terms, *[swap(sent[(j - 1) * size : j * size], j << (width + 1)) for j in order]
        )
        size = table.shape[0] // 4 if width > 1 else table.shape[0] // 2
        terms, sent = [table[:size]], table[size:]
    nodes = run_nodes(devices, rows, table, swap(table, devices // 2))
    pieces = [nodes]
    for take, width in groups[::-1]:
        pieces += [
            swap(piece, j << (width + 1))
            for j in ((3, 1, 2) if take == 2 else (1,))
            for piece in pieces
        ]
    own, own_key_value = run_own(devices, me, nodes, proj_weight)
    mine, theirs = run_partial(own, swap(own, 1), own_key_value, proj_weight, pieces[1:])
    return run_merge(mine, swap(theirs, 1), final_gain.reshape(1, D))


def solution(mesh):
    placed = (
        P(("groups", "blk"), None),
        P(),
        P(),
        P(("groups", "blk"), None),
        P(("groups", "blk")),
        P(("groups", "blk")),
        P(),
        P(),
    )
    return jax.shard_map(
        body, mesh=mesh, in_specs=placed, out_specs=P(("groups", "blk"), None), check_vma=False
    )
```

```python
import functools

import jax
import jax.numpy as jnp
from jax import lax
from jax.experimental import pallas as pl
from jax.experimental.pallas import tpu as pltpu
from jax.sharding import PartitionSpec as P

D = 768
HEADS = 12
S_DEV = 32
DH = 64
LANES = 128
GROUP_ROWS = 2 * S_DEV
COLS = D // LANES
TOTAL_ROWS = 16
CHUNK = COLS * GROUP_ROWS + TOTAL_ROWS
LANES_PER_GROUP = LANES // (GROUP_ROWS // TOTAL_ROWS)
MIB = 1024 * 1024


def digit_bits(devices):
    return max(1, (256 // devices).bit_length() - 1)


def total_bits(rows):
    return (4 * rows).bit_length()


def gelu(values):
    half = 0.5 * values
    return half + half * lax.erf(values * 0.7071067811865476)


def hidden_parts(ff):
    stops = [stop for stop in (768,) if stop < ff] + [ff]
    return [slice(start, stop) for start, stop in zip([0] + stops[:-1], stops)]


def points_kernel(
    devices, me_ref, x_hbm, hidden_hbm, output_hbm, owner_hbm, node_hbm, weight_hbm,
    send_ref, features_ref, kept_ref, tiles_ref, owner_ref, node_ref, weight_ref, x_ref, normed_ref, hidden_ref, output_ref, coeffs_ref, middle_ref, sems,
):
    rows = x_ref.shape[0]
    ff = hidden_ref.shape[1]
    parts = hidden_parts(ff)

    def hidden_copy(part):
        at = parts[part]
        return pltpu.make_async_copy(hidden_hbm.at[:, at], hidden_ref.at[:, at], sems.at[2 + part])

    x_copy = pltpu.make_async_copy(x_hbm, x_ref, sems.at[0])
    output_copy = pltpu.make_async_copy(output_hbm, output_ref, sems.at[1])
    index_copies = [
        pltpu.make_async_copy(source, target, sems.at[2 + len(parts) + i])
        for i, (source, target) in enumerate(
            ((owner_hbm, owner_ref), (node_hbm, node_ref), (weight_hbm, weight_ref))
        )
    ]
    for copy in index_copies:
        copy.start()
    x_copy.start()
    for part in range(len(parts)):
        hidden_copy(part).start()
    output_copy.start()

    chunks = devices // 4
    half = chunks * GROUP_ROWS
    me = me_ref[0]

    @pl.when(me >= 0)
    def _():
        for copy in index_copies:
            copy.wait()
        owner = owner_ref[...]
        near = (owner ^ me) & (devices // 2 - 1)
        row_of = (near // 2) * GROUP_ROWS + (owner // (devices // 2)) * S_DEV + node_ref[...]
        row_of = row_of + (near & 1) * half
        coeffs = jnp.where(
            row_of == lax.broadcasted_iota(jnp.int32, (2 * half, rows), 0), weight_ref[...], 0
        ).astype(jnp.float32)
        kept_ref[...] = coeffs[:half].astype(jnp.bfloat16)
        coeffs_ref[...] = coeffs[half:].astype(jnp.bfloat16)
        totals = jnp.sum(coeffs, axis=1, keepdims=True).astype(jnp.int32)
        shift = digit_bits(devices)
        digits = -(-total_bits(rows) // shift)
        lane = lax.broadcasted_iota(jnp.int32, (TOTAL_ROWS, LANES), 1)
        digit = lane % LANES_PER_GROUP
        held = jnp.where(digit < digits, digit * shift, 31)
        for chunk in range(2 * chunks):
            tile = jnp.zeros((TOTAL_ROWS, LANES), jnp.int32)
            for group in range(GROUP_ROWS // TOTAL_ROWS):
                start = chunk * GROUP_ROWS + group * TOTAL_ROWS
                value = jnp.broadcast_to(totals[start : start + TOTAL_ROWS], (TOTAL_ROWS, LANES))
                tile = jnp.where(lane // LANES_PER_GROUP == group, value, tile)
            tile = ((tile >> held) & ((1 << shift) - 1)).astype(jnp.float32).astype(jnp.bfloat16)
            if chunk < chunks:
                tiles_ref[chunk * TOTAL_ROWS : (chunk + 1) * TOTAL_ROWS, :] = tile
            else:
                end = (chunk - chunks + 1) * CHUNK
                send_ref[end - TOTAL_ROWS : end, :] = tile

    x_copy.wait()
    x = x_ref[...].astype(jnp.float32)
    scale = lax.rsqrt(jnp.mean(x * x, axis=-1, keepdims=True) + 1e-06)
    normed_ref[...] = (x * scale).astype(jnp.bfloat16)

    def one_part(part):
        at = parts[part]

        @pl.when(me > -2 - part)
        def _():
            hidden_copy(part).wait()
            middle_ref[:, at] = gelu(
                jnp.dot(normed_ref[...], hidden_ref[:, at], preferred_element_type=jnp.float32)
            ).astype(jnp.bfloat16)

    for part in range(len(parts)):
        one_part(part)
    output_copy.wait()
    sums = None
    half_rows = rows // 2
    for at in (slice(0, half_rows), slice(half_rows, rows)):
        features = (
            x_ref[at, :].astype(jnp.float32)
            + jnp.dot(middle_ref[at, :], output_ref[...], preferred_element_type=jnp.float32)
        ).astype(jnp.bfloat16)
        features_ref[at, :] = features
        term = jnp.dot(coeffs_ref[:, at], features, preferred_element_type=jnp.float32)
        sums = term if sums is None else sums + term
    store_table(send_ref, sums.astype(jnp.bfloat16))


def store_table(out_ref, sums):
    for first in range(0, sums.shape[0], GROUP_ROWS):
        for col in range(COLS):
            at = first // GROUP_ROWS * CHUNK + col * GROUP_ROWS
            out_ref[at : at + GROUP_ROWS, :] = sums[
                first : first + GROUP_ROWS, col * LANES : (col + 1) * LANES
            ]


def keep_kernel(features_ref, kept_ref, tiles_ref, out_ref):
    sums = jnp.dot(kept_ref[...], features_ref[...], preferred_element_type=jnp.float32)
    store_table(out_ref, sums.astype(jnp.bfloat16))
    for chunk in range(tiles_ref.shape[0] // TOTAL_ROWS):
        end = (chunk + 1) * CHUNK
        out_ref[end - TOTAL_ROWS : end, :] = tiles_ref[
            chunk * TOTAL_ROWS : (chunk + 1) * TOTAL_ROWS, :
        ]


def run_keep(features, kept, tiles):
    nodes, rows = kept.shape
    return pl.pallas_call(
        keep_kernel,
        out_shape=pltpu.VMEM((nodes // GROUP_ROWS * CHUNK, LANES), jnp.bfloat16),
        compiler_params=pltpu.CompilerParams(vmem_limit_bytes=8 * MIB + 16 * nodes * D),
        cost_estimate=pl.CostEstimate(
            flops=2 * nodes * rows * D, bytes_accessed=4 * nodes * D, transcendentals=0
        ),
        name="keep",
    )(*in_vmem(features, kept, tiles))


def run_points(devices, me, x, hidden_weight, output_weight, owner, node, weight):
    rows, ff = x.shape[0], hidden_weight.shape[1]
    nodes = devices * S_DEV
    out = pltpu.VMEM((devices // 4 * CHUNK, LANES), jnp.bfloat16)
    hbm = pl.BlockSpec(memory_space=pl.ANY)
    vmem = pl.BlockSpec(memory_space=pltpu.VMEM)
    in_hbm = [
        pltpu.with_memory_space_constraint(array, pltpu.HBM)
        for array in (x, hidden_weight, output_weight, owner, node, weight)
    ]
    return pl.pallas_call(
        functools.partial(points_kernel, devices),
        in_specs=[pl.BlockSpec(memory_space=pltpu.SMEM)] + [hbm] * 6,
        out_specs=[vmem] * 4,
        out_shape=[
            out,
            pltpu.VMEM((rows, D), jnp.bfloat16),
            pltpu.VMEM((nodes // 2, rows), jnp.bfloat16),
            pltpu.VMEM((devices // 4 * TOTAL_ROWS, LANES), jnp.bfloat16),
        ],
        scratch_shapes=[
            pltpu.VMEM((1, rows), jnp.int32),
            pltpu.VMEM((1, rows), jnp.int32),
            pltpu.VMEM((1, rows), jnp.int32),
            pltpu.VMEM((rows, D), jnp.bfloat16),
            pltpu.VMEM((rows, D), jnp.bfloat16),
            pltpu.VMEM((D, ff), jnp.bfloat16),
            pltpu.VMEM((ff, D), jnp.bfloat16),
            pltpu.VMEM((nodes // 2, rows), jnp.bfloat16),
            pltpu.VMEM((rows, ff), jnp.bfloat16),
            pltpu.SemaphoreType.DMA((5 + len(hidden_parts(ff)),)),
        ],
        compiler_params=pltpu.CompilerParams(vmem_limit_bytes=28 * MIB + 8 * nodes * D),
        name="points",
    )(me, *in_hbm)


def nodes_kernel(devices, rows, mine_ref, other_ref, out_ref):
    def part(start, size):
        at = slice(start, start + size)
        return mine_ref[at, :].astype(jnp.float32) + other_ref[at, :].astype(jnp.float32)

    shift = digit_bits(devices)
    digits = -(-total_bits(rows) // shift)
    lane = lax.broadcasted_iota(jnp.int32, (TOTAL_ROWS, LANES), 1)
    digit = lane % LANES_PER_GROUP
    worth = jnp.where(digit < digits, 1 << jnp.minimum(digit * shift, 30), 0).astype(jnp.float32)
    tile = part(COLS * GROUP_ROWS, TOTAL_ROWS) * worth
    totals = jnp.concatenate(
        [
            jnp.sum(jnp.where(lane // LANES_PER_GROUP == g, tile, 0.0), axis=1, keepdims=True)
            for g in range(GROUP_ROWS // TOTAL_ROWS)
        ],
        axis=0,
    )
    pooled = jnp.concatenate(
        [part(col * GROUP_ROWS, GROUP_ROWS) for col in range(COLS)], axis=1
    ) / (1.0 + totals)
    scale = lax.rsqrt(jnp.mean(pooled * pooled, axis=-1, keepdims=True) + 1e-06)
    out_ref[...] = (pooled * scale).astype(jnp.bfloat16)


def run_nodes(devices, rows, mine, other):
    return pl.pallas_call(
        functools.partial(nodes_kernel, devices, rows),
        out_shape=pltpu.VMEM((GROUP_ROWS, D), jnp.bfloat16),
        compiler_params=pltpu.CompilerParams(vmem_limit_bytes=8 * MIB),
        name="nodes",
    )(*in_vmem(mine, other))


def in_vmem(*arrays):
    return [pltpu.with_memory_space_constraint(array, pltpu.VMEM) for array in arrays]


def project(rows, proj_ref, start, size):
    return jnp.dot(
        rows, proj_ref[:, start : start + size], preferred_element_type=jnp.float32
    ).astype(jnp.bfloat16)


def own_kernel(devices, me_ref, nodes_ref, proj_ref, query_ref, key_value_ref):
    first = pl.multiple_of(me_ref[0] // (devices // 2) * S_DEV, S_DEV)
    query_ref[...] = project(nodes_ref[pl.ds(first, S_DEV), :], proj_ref, 0, D)
    key_value_ref[...] = project(nodes_ref[...], proj_ref, D, 2 * D)


def run_own(devices, me, nodes, proj_weight):
    return pl.pallas_call(
        functools.partial(own_kernel, devices),
        in_specs=[pl.BlockSpec(memory_space=pltpu.SMEM)]
        + [pl.BlockSpec(memory_space=pltpu.VMEM)] * 2,
        out_shape=[
            pltpu.VMEM((S_DEV, D), jnp.bfloat16),
            pltpu.VMEM((GROUP_ROWS, 2 * D), jnp.bfloat16),
        ],
        compiler_params=pltpu.CompilerParams(vmem_limit_bytes=12 * MIB),
        cost_estimate=pl.CostEstimate(
            flops=2 * (S_DEV + 2 * GROUP_ROWS) * D * D, bytes_accessed=6 * D * D, transcendentals=0
        ),
        name="own",
    )(me, *in_vmem(nodes, proj_weight))


def partial_kernel(own_ref, other_ref, own_key_value_ref, proj_ref, *refs):
    *pieces, mine_ref, theirs_ref, nodes_ref = refs
    start = 0
    for piece in pieces:
        nodes_ref[start : start + piece.shape[0], :] = piece[...]
        start += piece.shape[0]
    queries = jnp.concatenate([own_ref[...], other_ref[...]], axis=0)
    key_value = jnp.concatenate(
        [own_key_value_ref[...], project(nodes_ref[...], proj_ref, D, 2 * D)], axis=0
    )
    keys, values = key_value[:, :D], key_value[:, D:]
    rows = 2 * S_DEV
    lane = lax.broadcasted_iota(jnp.int32, (rows, LANES), 1)
    low = lane < DH
    stats = jnp.zeros((rows, LANES), jnp.float32)
    for pair in range(COLS):
        at = slice(pair * LANES, (pair + 1) * LANES)
        both = queries[:, at]
        zero = jnp.zeros_like(both)
        stacked = jnp.concatenate(
            [jnp.where(low, both, zero), jnp.where(low, zero, both)], axis=0
        )
        scores = lax.dot_general(
            stacked, keys[:, at], (((1,), (1,)), ((), ())), preferred_element_type=jnp.float32
        ) * (DH**-0.5)
        highest = jnp.max(scores, axis=-1, keepdims=True)
        exps = jnp.exp(scores - highest)
        total = jnp.sum(exps, axis=-1, keepdims=True)
        summed = jnp.dot(
            exps.astype(jnp.bfloat16), values[:, at], preferred_element_type=jnp.float32
        )
        for half in (0, 1):
            these = slice(half * rows, (half + 1) * rows)
            stats = jnp.where(lane == 2 * pair + half, highest[these], stats)
            stats = jnp.where(lane == DH + 2 * pair + half, total[these], stats)
        piece = jnp.where(low, summed[:rows], summed[rows:])
        mine_ref[:, at] = piece[:S_DEV]
        theirs_ref[:, at] = piece[S_DEV:]
    mine_ref[:, D:] = stats[:S_DEV]
    theirs_ref[:, D:] = stats[S_DEV:]


def run_partial(own, other, own_key_value, proj_weight, pieces):
    rows = sum(piece.shape[0] for piece in pieces)
    out = pltpu.VMEM((S_DEV, D + LANES), jnp.float32)
    return pl.pallas_call(
        partial_kernel,
        out_shape=[out, out],
        scratch_shapes=[pltpu.VMEM((rows, D), jnp.bfloat16)],
        compiler_params=pltpu.CompilerParams(vmem_limit_bytes=12 * MIB + 24 * rows * D),
        name="partial",
    )(*in_vmem(own, other, own_key_value, proj_weight, *pieces))


def merge_kernel(mine_ref, theirs_ref, gain_ref, out_ref):
    mine, theirs = mine_ref[:, D:], theirs_ref[:, D:]
    highest = jnp.maximum(mine, theirs)
    mine_scale, theirs_scale = jnp.exp(mine - highest), jnp.exp(theirs - highest)
    mine_total = pltpu.roll(mine, DH, 1)
    theirs_total = pltpu.roll(theirs, DH, 1)
    total = mine_total * mine_scale + theirs_total * theirs_scale
    mine_scale, theirs_scale = mine_scale / total, theirs_scale / total
    low = lax.broadcasted_iota(jnp.int32, (S_DEV, LANES), 1) < DH
    heads = []
    for pair in range(COLS):
        at = slice(pair * LANES, (pair + 1) * LANES)
        first, second = slice(2 * pair, 2 * pair + 1), slice(2 * pair + 1, 2 * pair + 2)
        heads.append(
            mine_ref[:, at] * jnp.where(low, mine_scale[:, first], mine_scale[:, second])
            + theirs_ref[:, at] * jnp.where(low, theirs_scale[:, first], theirs_scale[:, second])
        )
    attended = jnp.concatenate(heads, axis=1)
    scale = lax.rsqrt(jnp.mean(attended * attended, axis=-1, keepdims=True) + 1e-06)
    out_ref[...] = (attended * scale * gain_ref[...].astype(jnp.float32)).astype(jnp.bfloat16)


def run_merge(mine, theirs, gain):
    return pl.pallas_call(
        merge_kernel,
        out_shape=jax.ShapeDtypeStruct((S_DEV, D), jnp.bfloat16),
        compiler_params=pltpu.CompilerParams(vmem_limit_bytes=8 * MIB),
        name="merge",
    )(*in_vmem(mine, theirs), gain)


def add_up(first, *rest):
    total = first.astype(jnp.float32)
    for term in rest:
        total = total + term.astype(jnp.float32)
    return total.astype(jnp.bfloat16)


def body(
    points_in,
    hidden_weight,
    output_weight,
    point_owner,
    point_node,
    point_weight,
    proj_weight,
    final_gain,
):
    rows = points_in.shape[0]
    devices = lax.axis_size("blk")
    me = lax.axis_index("blk").astype(jnp.int32).reshape(1)

    def swap(array, flip):
        return lax.ppermute(array, "blk", [(i, i ^ flip) for i in range(devices)])

    send, *kept = run_points(
        devices,
        me,
        points_in,
        hidden_weight,
        output_weight,
        point_owner.reshape(1, rows),
        point_node.reshape(1, rows),
        point_weight.reshape(1, rows),
    )
    table = add_up(run_keep(*kept), swap(send, 1))
    groups = []
    width = (devices // 4).bit_length() - 1
    while width > 0:
        take = min(2, width)
        width -= take
        groups.append((take, width))
    for take, width in groups:
        size = (1 << width) * CHUNK
        parts = [table[j * size : (j + 1) * size] for j in range(1 << take)]
        order = (2, 1, 3) if take == 2 else (1,)
        table = add_up(parts[0], *[swap(parts[j], j << (width + 1)) for j in order])
    nodes = run_nodes(devices, rows, table, swap(table, devices // 2))
    pieces = [nodes]
    for take, width in groups[::-1]:
        pieces += [
            swap(piece, j << (width + 1))
            for j in ((3, 1, 2) if take == 2 else (1,))
            for piece in pieces
        ]
    own, own_key_value = run_own(devices, me, nodes, proj_weight)
    mine, theirs = run_partial(own, swap(own, 1), own_key_value, proj_weight, pieces[1:])
    return run_merge(mine, swap(theirs, 1), final_gain.reshape(1, D))


def solution(mesh):
    placed = (
        P(("groups", "blk"), None),
        P(),
        P(),
        P(("groups", "blk"), None),
        P(("groups", "blk")),
        P(("groups", "blk")),
        P(),
        P(),
    )
    return jax.shard_map(
        body, mesh=mesh, in_specs=placed, out_specs=P(("groups", "blk"), None), check_vma=False
    )
```

```python
import functools

import jax
import jax.numpy as jnp
from jax import lax
from jax.experimental import pallas as pl
from jax.experimental.pallas import tpu as pltpu
from jax.sharding import PartitionSpec as P

D = 768
HEADS = 12
S_DEV = 32
DH = 64
LANES = 128
GROUP_ROWS = 2 * S_DEV
COLS = D // LANES
TOTAL_ROWS = 16
CHUNK = COLS * GROUP_ROWS + TOTAL_ROWS
LANES_PER_GROUP = LANES // (GROUP_ROWS // TOTAL_ROWS)
MIB = 1024 * 1024


def digit_bits(devices):
    return max(1, (256 // devices).bit_length() - 1)


def total_bits(rows):
    return (4 * rows).bit_length()


def gelu(values):
    return 0.5 * values * (1.0 + lax.erf(values * 0.7071067811865476))


def hidden_parts(ff):
    stops = [stop for stop in (768,) if stop < ff] + [ff]
    return [slice(start, stop) for start, stop in zip([0] + stops[:-1], stops)]


def points_kernel(
    devices, me_ref, x_hbm, hidden_hbm, output_hbm, owner_hbm, node_hbm, weight_hbm,
    send_ref, features_ref, kept_ref, tiles_ref, owner_ref, node_ref, weight_ref, x_ref, normed_ref, hidden_ref, output_ref, coeffs_ref, middle_ref, sems,
):
    rows = x_ref.shape[0]
    ff = hidden_ref.shape[1]
    parts = hidden_parts(ff)

    def hidden_copy(part):
        at = parts[part]
        return pltpu.make_async_copy(hidden_hbm.at[:, at], hidden_ref.at[:, at], sems.at[2 + part])

    x_copy = pltpu.make_async_copy(x_hbm, x_ref, sems.at[0])
    output_copy = pltpu.make_async_copy(output_hbm, output_ref, sems.at[1])
    index_copies = [
        pltpu.make_async_copy(source, target, sems.at[2 + len(parts) + i])
        for i, (source, target) in enumerate(
            ((owner_hbm, owner_ref), (node_hbm, node_ref), (weight_hbm, weight_ref))
        )
    ]
    for copy in index_copies:
        copy.start()
    x_copy.start()
    for part in range(len(parts)):
        hidden_copy(part).start()
    output_copy.start()

    chunks = devices // 4
    half = chunks * GROUP_ROWS
    me = me_ref[0]

    @pl.when(me >= 0)
    def _():
        for copy in index_copies:
            copy.wait()
        owner = owner_ref[...]
        near = (owner ^ me) & (devices // 2 - 1)
        row_of = (near // 2) * GROUP_ROWS + (owner // (devices // 2)) * S_DEV + node_ref[...]
        row_of = row_of + (near & 1) * half
        coeffs = jnp.where(
            row_of == lax.broadcasted_iota(jnp.int32, (2 * half, rows), 0), weight_ref[...], 0
        ).astype(jnp.float32)
        kept_ref[...] = coeffs[:half].astype(jnp.bfloat16)
        coeffs_ref[...] = coeffs[half:].astype(jnp.bfloat16)
        totals = jnp.sum(coeffs, axis=1, keepdims=True).astype(jnp.int32)
        shift = digit_bits(devices)
        digits = -(-total_bits(rows) // shift)
        lane = lax.broadcasted_iota(jnp.int32, (TOTAL_ROWS, LANES), 1)
        digit = lane % LANES_PER_GROUP
        held = jnp.where(digit < digits, digit * shift, 31)
        for chunk in range(2 * chunks):
            tile = jnp.zeros((TOTAL_ROWS, LANES), jnp.int32)
            for group in range(GROUP_ROWS // TOTAL_ROWS):
                start = chunk * GROUP_ROWS + group * TOTAL_ROWS
                value = jnp.broadcast_to(totals[start : start + TOTAL_ROWS], (TOTAL_ROWS, LANES))
                tile = jnp.where(lane // LANES_PER_GROUP == group, value, tile)
            tile = ((tile >> held) & ((1 << shift) - 1)).astype(jnp.float32).astype(jnp.bfloat16)
            if chunk < chunks:
                tiles_ref[chunk * TOTAL_ROWS : (chunk + 1) * TOTAL_ROWS, :] = tile
            else:
                end = (chunk - chunks + 1) * CHUNK
                send_ref[end - TOTAL_ROWS : end, :] = tile

    x_copy.wait()
    x = x_ref[...].astype(jnp.float32)
    scale = lax.rsqrt(jnp.mean(x * x, axis=-1, keepdims=True) + 1e-06)
    normed_ref[...] = (x * scale).astype(jnp.bfloat16)

    def one_part(part):
        at = parts[part]

        @pl.when(me > -2 - part)
        def _():
            hidden_copy(part).wait()
            middle_ref[:, at] = gelu(
                jnp.dot(normed_ref[...], hidden_ref[:, at], preferred_element_type=jnp.float32)
            ).astype(jnp.bfloat16)

    for part in range(len(parts)):
        one_part(part)
    output_copy.wait()
    sums = None
    half_rows = rows // 2
    for at in (slice(0, half_rows), slice(half_rows, rows)):
        features = (
            x_ref[at, :].astype(jnp.float32)
            + jnp.dot(middle_ref[at, :], output_ref[...], preferred_element_type=jnp.float32)
        ).astype(jnp.bfloat16)
        features_ref[at, :] = features
        term = jnp.dot(coeffs_ref[:, at], features, preferred_element_type=jnp.float32)
        sums = term if sums is None else sums + term
    store_table(send_ref, sums.astype(jnp.bfloat16))


def store_table(out_ref, sums):
    for first in range(0, sums.shape[0], GROUP_ROWS):
        for col in range(COLS):
            at = first // GROUP_ROWS * CHUNK + col * GROUP_ROWS
            out_ref[at : at + GROUP_ROWS, :] = sums[
                first : first + GROUP_ROWS, col * LANES : (col + 1) * LANES
            ]


def keep_kernel(features_ref, kept_ref, tiles_ref, out_ref):
    sums = jnp.dot(kept_ref[...], features_ref[...], preferred_element_type=jnp.float32)
    store_table(out_ref, sums.astype(jnp.bfloat16))
    for chunk in range(tiles_ref.shape[0] // TOTAL_ROWS):
        end = (chunk + 1) * CHUNK
        out_ref[end - TOTAL_ROWS : end, :] = tiles_ref[
            chunk * TOTAL_ROWS : (chunk + 1) * TOTAL_ROWS, :
        ]


def run_keep(features, kept, tiles):
    nodes, rows = kept.shape
    return pl.pallas_call(
        keep_kernel,
        out_shape=pltpu.VMEM((nodes // GROUP_ROWS * CHUNK, LANES), jnp.bfloat16),
        compiler_params=pltpu.CompilerParams(vmem_limit_bytes=8 * MIB + 16 * nodes * D),
        cost_estimate=pl.CostEstimate(
            flops=2 * nodes * rows * D, bytes_accessed=4 * nodes * D, transcendentals=0
        ),
        name="keep",
    )(*in_vmem(features, kept, tiles))


def run_points(devices, me, x, hidden_weight, output_weight, owner, node, weight):
    rows, ff = x.shape[0], hidden_weight.shape[1]
    nodes = devices * S_DEV
    out = pltpu.VMEM((devices // 4 * CHUNK, LANES), jnp.bfloat16)
    hbm = pl.BlockSpec(memory_space=pl.ANY)
    vmem = pl.BlockSpec(memory_space=pltpu.VMEM)
    in_hbm = [
        pltpu.with_memory_space_constraint(array, pltpu.HBM)
        for array in (x, hidden_weight, output_weight, owner, node, weight)
    ]
    return pl.pallas_call(
        functools.partial(points_kernel, devices),
        in_specs=[pl.BlockSpec(memory_space=pltpu.SMEM)] + [hbm] * 6,
        out_specs=[vmem] * 4,
        out_shape=[
            out,
            pltpu.VMEM((rows, D), jnp.bfloat16),
            pltpu.VMEM((nodes // 2, rows), jnp.bfloat16),
            pltpu.VMEM((devices // 4 * TOTAL_ROWS, LANES), jnp.bfloat16),
        ],
        scratch_shapes=[
            pltpu.VMEM((1, rows), jnp.int32),
            pltpu.VMEM((1, rows), jnp.int32),
            pltpu.VMEM((1, rows), jnp.int32),
            pltpu.VMEM((rows, D), jnp.bfloat16),
            pltpu.VMEM((rows, D), jnp.bfloat16),
            pltpu.VMEM((D, ff), jnp.bfloat16),
            pltpu.VMEM((ff, D), jnp.bfloat16),
            pltpu.VMEM((nodes // 2, rows), jnp.bfloat16),
            pltpu.VMEM((rows, ff), jnp.bfloat16),
            pltpu.SemaphoreType.DMA((5 + len(hidden_parts(ff)),)),
        ],
        compiler_params=pltpu.CompilerParams(vmem_limit_bytes=28 * MIB + 8 * nodes * D),
        name="points",
    )(me, *in_hbm)


def nodes_kernel(devices, rows, mine_ref, other_ref, out_ref):
    def part(start, size):
        at = slice(start, start + size)
        return mine_ref[at, :].astype(jnp.float32) + other_ref[at, :].astype(jnp.float32)

    shift = digit_bits(devices)
    digits = -(-total_bits(rows) // shift)
    lane = lax.broadcasted_iota(jnp.int32, (TOTAL_ROWS, LANES), 1)
    digit = lane % LANES_PER_GROUP
    worth = jnp.where(digit < digits, 1 << jnp.minimum(digit * shift, 30), 0).astype(jnp.float32)
    tile = part(COLS * GROUP_ROWS, TOTAL_ROWS) * worth
    totals = jnp.concatenate(
        [
            jnp.sum(jnp.where(lane // LANES_PER_GROUP == g, tile, 0.0), axis=1, keepdims=True)
            for g in range(GROUP_ROWS // TOTAL_ROWS)
        ],
        axis=0,
    )
    pooled = jnp.concatenate(
        [part(col * GROUP_ROWS, GROUP_ROWS) for col in range(COLS)], axis=1
    ) / (1.0 + totals)
    scale = lax.rsqrt(jnp.mean(pooled * pooled, axis=-1, keepdims=True) + 1e-06)
    out_ref[...] = (pooled * scale).astype(jnp.bfloat16)


def run_nodes(devices, rows, mine, other):
    return pl.pallas_call(
        functools.partial(nodes_kernel, devices, rows),
        out_shape=pltpu.VMEM((GROUP_ROWS, D), jnp.bfloat16),
        compiler_params=pltpu.CompilerParams(vmem_limit_bytes=8 * MIB),
        name="nodes",
    )(*in_vmem(mine, other))


def in_vmem(*arrays):
    return [pltpu.with_memory_space_constraint(array, pltpu.VMEM) for array in arrays]


def project(rows, proj_ref, start, size):
    return jnp.dot(
        rows, proj_ref[:, start : start + size], preferred_element_type=jnp.float32
    ).astype(jnp.bfloat16)


def own_kernel(devices, me_ref, nodes_ref, proj_ref, query_ref, key_value_ref):
    first = pl.multiple_of(me_ref[0] // (devices // 2) * S_DEV, S_DEV)
    query_ref[...] = project(nodes_ref[pl.ds(first, S_DEV), :], proj_ref, 0, D)
    key_value_ref[...] = project(nodes_ref[...], proj_ref, D, 2 * D)


def run_own(devices, me, nodes, proj_weight):
    return pl.pallas_call(
        functools.partial(own_kernel, devices),
        in_specs=[pl.BlockSpec(memory_space=pltpu.SMEM)]
        + [pl.BlockSpec(memory_space=pltpu.VMEM)] * 2,
        out_shape=[
            pltpu.VMEM((S_DEV, D), jnp.bfloat16),
            pltpu.VMEM((GROUP_ROWS, 2 * D), jnp.bfloat16),
        ],
        compiler_params=pltpu.CompilerParams(vmem_limit_bytes=12 * MIB),
        cost_estimate=pl.CostEstimate(
            flops=2 * (S_DEV + 2 * GROUP_ROWS) * D * D, bytes_accessed=6 * D * D, transcendentals=0
        ),
        name="own",
    )(me, *in_vmem(nodes, proj_weight))


def partial_kernel(own_ref, other_ref, own_key_value_ref, proj_ref, *refs):
    *pieces, mine_ref, theirs_ref, nodes_ref = refs
    start = 0
    for piece in pieces:
        nodes_ref[start : start + piece.shape[0], :] = piece[...]
        start += piece.shape[0]
    queries = jnp.concatenate([own_ref[...], other_ref[...]], axis=0)
    key_value = jnp.concatenate(
        [own_key_value_ref[...], project(nodes_ref[...], proj_ref, D, 2 * D)], axis=0
    )
    keys, values = key_value[:, :D], key_value[:, D:]
    rows = 2 * S_DEV
    lane = lax.broadcasted_iota(jnp.int32, (rows, LANES), 1)
    low = lane < DH
    stats = jnp.zeros((rows, LANES), jnp.float32)
    for pair in range(COLS):
        at = slice(pair * LANES, (pair + 1) * LANES)
        both = queries[:, at]
        zero = jnp.zeros_like(both)
        stacked = jnp.concatenate(
            [jnp.where(low, both, zero), jnp.where(low, zero, both)], axis=0
        )
        scores = lax.dot_general(
            stacked, keys[:, at], (((1,), (1,)), ((), ())), preferred_element_type=jnp.float32
        ) * (DH**-0.5)
        highest = jnp.max(scores, axis=-1, keepdims=True)
        exps = jnp.exp(scores - highest)
        total = jnp.sum(exps, axis=-1, keepdims=True)
        summed = jnp.dot(
            exps.astype(jnp.bfloat16), values[:, at], preferred_element_type=jnp.float32
        )
        for half in (0, 1):
            these = slice(half * rows, (half + 1) * rows)
            stats = jnp.where(lane == 2 * pair + half, highest[these], stats)
            stats = jnp.where(lane == DH + 2 * pair + half, total[these], stats)
        piece = jnp.where(low, summed[:rows], summed[rows:])
        mine_ref[:, at] = piece[:S_DEV]
        theirs_ref[:, at] = piece[S_DEV:]
    mine_ref[:, D:] = stats[:S_DEV]
    theirs_ref[:, D:] = stats[S_DEV:]


def run_partial(own, other, own_key_value, proj_weight, pieces):
    rows = sum(piece.shape[0] for piece in pieces)
    out = pltpu.VMEM((S_DEV, D + LANES), jnp.float32)
    return pl.pallas_call(
        partial_kernel,
        out_shape=[out, out],
        scratch_shapes=[pltpu.VMEM((rows, D), jnp.bfloat16)],
        compiler_params=pltpu.CompilerParams(vmem_limit_bytes=12 * MIB + 24 * rows * D),
        name="partial",
    )(*in_vmem(own, other, own_key_value, proj_weight, *pieces))


def merge_kernel(mine_ref, theirs_ref, gain_ref, out_ref):
    mine, theirs = mine_ref[:, D:], theirs_ref[:, D:]
    highest = jnp.maximum(mine, theirs)
    mine_scale, theirs_scale = jnp.exp(mine - highest), jnp.exp(theirs - highest)
    mine_total = pltpu.roll(mine, DH, 1)
    theirs_total = pltpu.roll(theirs, DH, 1)
    total = mine_total * mine_scale + theirs_total * theirs_scale
    mine_scale, theirs_scale = mine_scale / total, theirs_scale / total
    low = lax.broadcasted_iota(jnp.int32, (S_DEV, LANES), 1) < DH
    heads = []
    for pair in range(COLS):
        at = slice(pair * LANES, (pair + 1) * LANES)
        first, second = slice(2 * pair, 2 * pair + 1), slice(2 * pair + 1, 2 * pair + 2)
        heads.append(
            mine_ref[:, at] * jnp.where(low, mine_scale[:, first], mine_scale[:, second])
            + theirs_ref[:, at] * jnp.where(low, theirs_scale[:, first], theirs_scale[:, second])
        )
    attended = jnp.concatenate(heads, axis=1)
    scale = lax.rsqrt(jnp.mean(attended * attended, axis=-1, keepdims=True) + 1e-06)
    out_ref[...] = (attended * scale * gain_ref[...].astype(jnp.float32)).astype(jnp.bfloat16)


def run_merge(mine, theirs, gain):
    return pl.pallas_call(
        merge_kernel,
        out_shape=jax.ShapeDtypeStruct((S_DEV, D), jnp.bfloat16),
        compiler_params=pltpu.CompilerParams(vmem_limit_bytes=8 * MIB),
        name="merge",
    )(*in_vmem(mine, theirs), gain)


def add_up(first, *rest):
    total = first.astype(jnp.float32)
    for term in rest:
        total = total + term.astype(jnp.float32)
    return total.astype(jnp.bfloat16)


def body(
    points_in,
    hidden_weight,
    output_weight,
    point_owner,
    point_node,
    point_weight,
    proj_weight,
    final_gain,
):
    rows = points_in.shape[0]
    devices = lax.axis_size("blk")
    me = lax.axis_index("blk").astype(jnp.int32).reshape(1)

    def swap(array, flip):
        return lax.ppermute(array, "blk", [(i, i ^ flip) for i in range(devices)])

    send, *kept = run_points(
        devices,
        me,
        points_in,
        hidden_weight,
        output_weight,
        point_owner.reshape(1, rows),
        point_node.reshape(1, rows),
        point_weight.reshape(1, rows),
    )
    table = add_up(run_keep(*kept), swap(send, 1))
    groups = []
    width = (devices // 4).bit_length() - 1
    while width > 0:
        take = min(2, width)
        width -= take
        groups.append((take, width))
    for take, width in groups:
        size = (1 << width) * CHUNK
        parts = [table[j * size : (j + 1) * size] for j in range(1 << take)]
        order = (2, 1, 3) if take == 2 else (1,)
        table = add_up(parts[0], *[swap(parts[j], j << (width + 1)) for j in order])
    nodes = run_nodes(devices, rows, table, swap(table, devices // 2))
    pieces = [nodes]
    for take, width in groups[::-1]:
        pieces += [
            swap(piece, j << (width + 1))
            for j in ((1, 3, 2) if take == 2 else (1,))
            for piece in pieces
        ]
    own, own_key_value = run_own(devices, me, nodes, proj_weight)
    mine, theirs = run_partial(own, swap(own, 1), own_key_value, proj_weight, pieces[1:])
    return run_merge(mine, swap(theirs, 1), final_gain.reshape(1, D))


def solution(mesh):
    placed = (
        P(("groups", "blk"), None),
        P(),
        P(),
        P(("groups", "blk"), None),
        P(("groups", "blk")),
        P(("groups", "blk")),
        P(),
        P(),
    )
    return jax.shard_map(
        body, mesh=mesh, in_specs=placed, out_specs=P(("groups", "blk"), None), check_vma=False
    )
```
